256 devices in a mesh: tm: 16 (over y_hi, x, core), rows: 16 (over z, y_lo).
Axes of the slice: x: 4, y: 4 (y_hi: 2, y_lo: 2; y = y_hi * 2 + y_lo), z: 8, core: 2. Of those that a mesh axis runs over, the one named last changes fastest.
Arguments:
- inputs: bfloat16 [16, 64, 120, 1024], P('tm', 'rows'), may hold values from -6 to 6
- hidden_one: bfloat16 [16, 64, 120, 256], P('tm', 'rows'), as said below
- hidden_two: bfloat16 [16, 64, 120, 256], P('tm', 'rows'), as said below
- outputs: bfloat16 [16, 64, 120, 1024], P('tm', 'rows'), as said below
- cotangent: bfloat16 [16, 64, 120, 1024], P('tm', 'rows'), may hold values from -6 to 6
- w_in: bfloat16 [1024, 256], replicated, may hold values from -0.1875 to 0.1875
- w_mid: bfloat16 [3, 3, 256, 256], replicated, may hold values from -0.125 to 0.125
- w_out: bfloat16 [256, 1024], replicated, may hold values from -0.375 to 0.375
Outputs:
- grad_inputs: bfloat16 [16, 64, 120, 1024], P('tm', 'rows')
- grad_w_in: float32 [1024, 256], P(('tm', 'rows'))
- grad_w_mid: float32 [3, 3, 65536], P(None, None, ('tm', 'rows'))
- grad_w_out: float32 [256, 1024], P(None, ('tm', 'rows'))
- grad_b_hidden: float32 [512], P(('tm', 'rows'))
- grad_b_out: float32 [1024], P(('tm', 'rows'))
The draws below stay inside these ranges and needn't reach their ends.
Inputs may be any that keep to these rules, and one draw needn't show every extreme that they name: `hidden_one`: rectified values: zero in about half the entries, positive elsewhere. `hidden_two`: rectified values: zero in about half the entries, positive elsewhere. `outputs`: rectified values: zero in about half the entries, positive elsewhere.
All inputs are finite; a program needn't handle non-finite values.
Results may differ from the reference program's by a relative error of at most 0.013.
Values may be sent and summed in bfloat16 or wider, within the bound.
A program may use at most 384 MiB of HBM per device.

```python
import jax
import jax.numpy as jnp
from jax import lax

C = 1024
MID = 256
W = 120
F = 16
H = 64


def draw_hidden_one(key, part):
    key = jax.random.fold_in(key, 11)
    values = jax.random.normal(key, (F, H, W, MID), jnp.float32)
    return jnp.maximum(values, 0.0).astype(jnp.bfloat16)


def draw_hidden_two(key, part):
    key = jax.random.fold_in(key, 23)
    values = jax.random.normal(key, (F, H, W, MID), jnp.float32)
    return jnp.maximum(values, 0.0).astype(jnp.bfloat16)


def draw_outputs(key, part):
    key = jax.random.fold_in(key, 37)
    values = jax.random.normal(key, (F, H, W, C), jnp.float32)
    return jnp.maximum(values, 0.0).astype(jnp.bfloat16)


def raised(drawn, stream_key, source, target, blocks, factor):
    def block_of(position):
        return (jnp.arange(drawn.shape[position]) // (drawn.shape[position] // blocks)).reshape((-1,) + (1,) * (drawn.ndim - 1 - position))

    one_side = jax.random.permutation(stream_key, blocks)[block_of(target)]
    other_side = (block_of(target) + blocks // 2) % blocks
    return jnp.where((block_of(source) == one_side) | (block_of(source) == other_side), factor * drawn, drawn)


def shard_levels(rng, extent, cuts, smallest, largest):
    def one(dim, blocks):
        steps = jax.random.uniform(jax.random.fold_in(jax.random.fold_in(rng, 6), dim), (blocks,), jnp.float32, smallest / len(cuts), largest / len(cuts))
        return jnp.repeat(jnp.exp(steps), extent[dim] // blocks).reshape((-1,) + (1,) * (len(extent) - dim - 1))

    gain = one(*cuts[0])
    for cut in cuts[1:]:
        gain = gain * one(*cut)
    return gain


def scatter_about(key, shape, scale, limit, split=(), dtype=jnp.bfloat16):
    gain = shard_levels(key, shape, split, -0.22, 0.18) if split else 1.0
    drawn = jax.random.normal(key, shape, jnp.float32) * scale * gain
    return jnp.minimum(jnp.maximum(drawn, -limit), limit).astype(dtype)


def gaussian_with(stream_key, extent, spread, reach, shards, heavy, held_as=jnp.bfloat16):
    result = spread * jax.random.normal(stream_key, extent, jnp.float32)
    if shards:
        result = result * shard_levels(stream_key, extent, shards, -0.22, 0.18)
    return jnp.clip(raised(result, jax.random.fold_in(stream_key, 3), *heavy), -reach, reach).astype(held_as)


def setup_inputs(seed: int = 0) -> dict:
    streams_of = jax.random.split(jax.random.key(seed), 9)
    inputs = scatter_about(streams_of[0], (F, H, W, C), 1.0, 6.0, ((0, 16), (1, 16)))
    hidden_one = draw_hidden_one(jax.random.fold_in(streams_of[8], 71), 0)
    hidden_two = draw_hidden_two(jax.random.fold_in(streams_of[8], 71), 0)
    outputs = draw_outputs(jax.random.fold_in(streams_of[8], 71), 0)
    cotangent = gaussian_with(streams_of[4], (F, H, W, C), 1.0, 6.0, ((0, 16), (1, 16)), (0, 3, 16, 2.0))
    w_in = scatter_about(streams_of[5], (C, MID), C ** -0.5, 0.1875)
    w_mid = scatter_about(streams_of[6], (3, 3, MID, MID), (9 * MID) ** -0.5, 0.125)
    w_out = scatter_about(streams_of[7], (MID, C), MID ** -0.5, 0.375)
    return {"inputs": inputs, "hidden_one": hidden_one, "hidden_two": hidden_two, "outputs": outputs, "cotangent": cotangent, "w_in": w_in, "w_mid": w_mid, "w_out": w_out}


def reference(inputs, hidden_one, hidden_two, outputs, cotangent, w_in, w_mid, w_out):
    chans = inputs.shape[-1]
    mids = hidden_one.shape[-1]
    shifted_width = chans // 8
    height = inputs.shape[1]
    width = inputs.shape[2]
    out_grad = jnp.where(outputs > 0, cotangent, jnp.zeros_like(cotangent))
    blank = jnp.zeros_like(inputs[:1, :, :, :shifted_width])
    previous = jnp.concatenate([blank, inputs[:-1, :, :, :shifted_width]], 0)
    following = jnp.concatenate([inputs[1:, :, :, shifted_width:2 * shifted_width], blank], 0)
    shifted = jnp.concatenate([previous, following, inputs[:, :, :, 2 * shifted_width:]], -1)

    def frame_step(totals, frame_item):
        shift_t, one_t, two_t, grad_t = frame_item
        grad_flat = grad_t.reshape(-1, chans)
        two_flat = two_t.reshape(-1, mids)
        d_out = jnp.dot(two_flat.T, grad_flat, preferred_element_type=jnp.float32)
        b_out = jnp.sum(grad_flat.astype(jnp.float32), 0)
        back_two = jnp.dot(grad_flat, w_out.T, preferred_element_type=jnp.float32)
        mid_grad = jnp.where(two_flat > 0, back_two, 0.0).astype(jnp.bfloat16)
        mid_map = mid_grad.reshape(height, width, mids)
        padded_one = jnp.pad(one_t, ((1, 1), (1, 1), (0, 0)))
        padded_mid = jnp.pad(mid_map, ((1, 1), (1, 1), (0, 0)))
        kernel_rows = []
        back_one = jnp.zeros((height * width, mids), jnp.float32)
        for row_off in range(3):
            kernel_cols = []
            for col_off in range(3):
                window = padded_one[row_off:row_off + height, col_off:col_off + width].reshape(-1, mids)
                kernel_cols.append(jnp.dot(window.T, mid_grad, preferred_element_type=jnp.float32))
                source = padded_mid[2 - row_off:2 - row_off + height, 2 - col_off:2 - col_off + width].reshape(-1, mids)
                back_one = back_one + jnp.dot(source, w_mid[row_off, col_off].T, preferred_element_type=jnp.float32)
            kernel_rows.append(jnp.stack(kernel_cols, 0))
        d_mid = jnp.stack(kernel_rows, 0)
        b_mid = jnp.sum(mid_grad.astype(jnp.float32), 0)
        first_grad = jnp.where(one_t.reshape(-1, mids) > 0, back_one, 0.0).astype(jnp.bfloat16)
        d_in = jnp.dot(shift_t.reshape(-1, chans).T, first_grad, preferred_element_type=jnp.float32)
        b_in = jnp.sum(first_grad.astype(jnp.float32), 0)
        sums = (totals[0] + d_in, totals[1] + d_mid, totals[2] + d_out,
                totals[3] + b_in, totals[4] + b_mid, totals[5] + b_out)
        return sums, first_grad.reshape(height, width, mids)

    start = (jnp.zeros((chans, mids), jnp.float32), jnp.zeros((3, 3, mids, mids), jnp.float32),
             jnp.zeros((mids, chans), jnp.float32), jnp.zeros((mids,), jnp.float32),
             jnp.zeros((mids,), jnp.float32), jnp.zeros((chans,), jnp.float32))
    totals, first_all = lax.scan(frame_step, start, (shifted, hidden_one, hidden_two, out_grad))
    blank_mid = jnp.zeros_like(first_all[:1])
    first_prev = jnp.concatenate([blank_mid, first_all[:-1]], 0)
    first_next = jnp.concatenate([first_all[1:], blank_mid], 0)

    def frame_input(frame_item):
        grad_t, prev_t, here_t, next_t = frame_item
        part_early = jnp.dot(next_t.reshape(-1, mids), w_in[:shifted_width].T, preferred_element_type=jnp.float32)
        part_late = jnp.dot(prev_t.reshape(-1, mids), w_in[shifted_width:2 * shifted_width].T, preferred_element_type=jnp.float32)
        part_rest = jnp.dot(here_t.reshape(-1, mids), w_in[2 * shifted_width:].T, preferred_element_type=jnp.float32)
        back = jnp.concatenate([part_early, part_late, part_rest], -1)
        total = grad_t.reshape(-1, chans).astype(jnp.float32) + back
        return total.astype(jnp.bfloat16).reshape(height, width, chans)

    grad_inputs = lax.map(frame_input, (out_grad, first_prev, first_all, first_next))
    kernel_flat = totals[1].reshape(3, 3, mids * mids)
    bias_hidden = jnp.concatenate([totals[3], totals[4]], 0)
    return (grad_inputs, totals[0], kernel_flat, totals[2], bias_hidden, totals[5])
```

```python
import jax
import jax.numpy as jnp
from jax import lax
from jax.experimental import pallas as pl
from jax.experimental.pallas import tpu as pltpu
from jax.sharding import PartitionSpec as P

F32 = jnp.float32
BF16 = jnp.bfloat16
MESH = pl.DeviceIdType.MESH

BAND = 4
W = 120
WP = 128
NP = BAND * WP
C = 1024
M = 256
E = C // 8
PIECES = ((2, 2, 8), (5, 4, 24), (2, 3, 16))


def dot_t0(a, b):
    return lax.dot_general(a, b, (((0,), (0,)), ((), ())), preferred_element_type=F32)


def dot_t1(a, b):
    return lax.dot_general(a, b, (((1,), (1,)), ((), ())), preferred_element_type=F32)


def pad_rows(value):
    return jnp.concatenate([value, jnp.zeros((WP - W, value.shape[1]), F32)], 0).astype(BF16)


def kernel(
    inp, h1, h2, outp, cot, w_in, w_mid, w_out,
    gi_out, f0_out, f1_out, f2_out,
    inp_v, h1_v, h2_v, outp_v, cot_v, win_v, wmid_v, wout_v,
    og, h2p, h1x, m3, shifted, first, sprev, snext, h1up, h1dn, mup, mdn, mid_s,
    prod_e, prod_l, got_e, got_l, gi, back, d0, kf, d2, bo, bh,
    cs0, cr0, a1s0, a1r0, b1s0, b1r0, a2s0, a2r0, b2s0, b2r0, zs0, zr0,
    cs1, cr1, a1s1, a1r1, b1s1, b1r1, a2s1, a2r1, b2s1, b2r1, zs1, zr1,
    cs2, cr2, a1s2, a1r2, b1s2, b1r2, a2s2, a2r2, b2s2, b2r2, zs2, zr2,
    load_sem, send_sem, recv_sem,
):
    tm = lax.axis_index("tm")
    rows = lax.axis_index("rows")
    n_tm = lax.axis_size("tm")
    n_rows = lax.axis_size("rows")
    core = tm % 2
    mx = (tm // 2) % 4
    my = (tm // 8) * 2 + rows % 2
    mz = rows // 2

    def at(x, y, z, c):
        return (((y // 2) * 4 + x) * 2 + c, z * 2 + y % 2)

    sibling = at(mx, my, mz, 1 - core)
    x_peer = [at((mx + k) % 4, my, mz, core) for k in range(1, 4)]
    y_peer = [at(mx, (my + k) % 4, mz, core) for k in range(1, 4)]
    z_peer = [at(mx, my, (mz + k) % 8, core) for k in range(1, 8)]
    tm_next = ((tm + 1) % n_tm, rows)
    tm_prev = ((tm + n_tm - 1) % n_tm, rows)
    row_next = (tm, (rows + 1) % n_rows)
    row_prev = (tm, (rows + n_rows - 1) % n_rows)

    loads = []
    for i, (src, dst) in enumerate(
        ((outp, outp_v), (cot, cot_v), (w_out, wout_v), (h2, h2_v), (h1, h1_v), (w_mid, wmid_v), (inp, inp_v), (w_in, win_v))
    ):
        copy = pltpu.make_async_copy(src, dst, load_sem.at[i])
        copy.start()
        loads.append(copy)

    barrier = pltpu.get_barrier_semaphore()
    partners = [sibling, *x_peer, *y_peer, *z_peer, tm_next, tm_prev, row_next, row_prev]
    for peer in partners:
        pl.semaphore_signal(barrier, inc=1, device_id=peer, device_id_type=MESH)

    counter = [0]

    def send(src, dst, peer):
        i = counter[0]
        counter[0] += 1
        copy = pltpu.make_async_remote_copy(
            src_ref=src, dst_ref=dst, send_sem=send_sem.at[i], recv_sem=recv_sem.at[i],
            device_id=peer, device_id_type=MESH,
        )
        copy.start()
        return copy

    for copy in loads[:4]:
        copy.wait()
    for r in range(BAND):
        grad = jnp.where(outp_v[r].astype(F32) > 0, cot_v[r].astype(F32), 0.0)
        og[r * WP : (r + 1) * WP, :] = pad_rows(grad)
        h2p[r * WP : (r + 1) * WP, :] = pad_rows(h2_v[r].astype(F32))
    mid32 = jnp.where(h2p[...].astype(F32) > 0, dot_t1(og[...], wout_v[...]), 0.0)
    mid_s[...] = mid32.astype(BF16)
    m3[WP : WP + NP, 0:M] = pltpu.roll(mid32, NP - 1, 0).astype(BF16)
    m3[WP : WP + NP, M : 2 * M] = mid_s[...]
    m3[WP : WP + NP, 2 * M : 3 * M] = pltpu.roll(mid32, 1, 0).astype(BF16)
    ones = jnp.ones((NP, WP), BF16)
    grad = dot_t0(og[...], h2p[...])
    for h in range(2):
        d0[h] = grad[:, h * 128 : (h + 1) * 128].reshape(16, 64, 128)
    bo[...] = dot_t0(og[...], ones).reshape(16, 64, WP)
    bh[8:16] = dot_t0(mid_s[...], ones).reshape(8, 32, WP)

    pl.semaphore_wait(barrier, len(partners))
    mid_down = send(mid_s.at[pl.ds((BAND - 1) * WP, WP)], mup, row_next)
    mid_up = send(mid_s.at[pl.ds(0, WP)], mdn, row_prev)
    one_down = send(h1.at[BAND - 1], h1up, row_next)
    one_up = send(h1.at[0], h1dn, row_prev)
    in_next = send(inp.at[:, :, pl.ds(0, E)], sprev, tm_next)
    in_prev = send(inp.at[:, :, pl.ds(E, E)], snext, tm_prev)

    def slab(piece, t, low, s):
        if piece == 1:
            parts = [kf[2 * s + h, t, pl.ds(low, 8, stride=2), :] for h in range(2)]
        elif s < 4:
            held = d0 if piece == 0 else d2
            parts = [held[h, t, pl.ds(4 * low + s, 8, stride=8), :] for h in range(2)]
        else:
            lane = lax.broadcasted_iota(jnp.int32, (8, 128), 1)
            total = jnp.zeros((8, 128), F32)
            for j in range(4):
                total = jnp.where(lane == j, bo[t, pl.ds(4 * low + j, 8, stride=8), :], total)
            for j in range(2):
                total = jnp.where(lane == 4 + j, bh[t, pl.ds(2 * low + j, 8, stride=4), :], total)
            parts = [total, jnp.zeros((8, 128), F32)]
        return jnp.concatenate(parts, 0)

    def two_terms(value):
        total = value[0:8] + value[8:16]
        head = total.astype(BF16).astype(F32)
        return jnp.concatenate([head, total - head], 0)

    bufs = (
        (cs0, cr0, a1s0, a1r0, b1s0, b1r0, a2s0, a2r0, b2s0, b2r0, zs0, zr0),
        (cs1, cr1, a1s1, a1r1, b1s1, b1r1, a2s1, a2r1, b2s1, b2r1, zs1, zr1),
        (cs2, cr2, a1s2, a1r2, b1s2, b1r2, a2s2, a2r2, b2s2, b2r2, zs2, zr2),
    )

    def core_phase(p):
        na, nb, _ = PIECES[p]
        cs, cr = bufs[p][:2]

        def body(x, carry):
            for y in range(4):
                t = ((y // 2) * 4 + x) * 2 + (1 - core)
                for s in range(na + nb):
                    value = slab(p, t, y % 2, s)
                    if p == 2 and s == 4:
                        value = two_terms(value)
                    cs[x, y, s] = value.astype(BF16)
            return carry

        lax.fori_loop(0, 4, body, 0)
        return [send(cs, cr, sibling)]

    def first_phase(p, copies):
        na, nb, _ = PIECES[p]
        cs, cr, a1s, a1r, b1s, b1r = bufs[p][:6]
        for copy in copies:
            copy.wait()

        def body(x, carry):
            for y in range(4):
                t = ((y // 2) * 4 + x) * 2 + core
                for s in range(na + nb):
                    value = slab(p, t, y % 2, s) + cr[x, y, s].astype(F32)
                    if p == 2 and s == 4:
                        value = two_terms(value)
                    if s < na:
                        a1s[x, y, s] = value.astype(BF16)
                    else:
                        b1s[y, x, s - na] = value.astype(BF16)
            return carry

        lax.fori_loop(0, 4, body, 0)
        out = []
        for k in (2, 1, 3):
            out.append(send(a1s.at[(mx + k) % 4], a1r.at[k - 1], x_peer[k - 1]))
            out.append(send(b1s.at[(my + k) % 4], b1r.at[k - 1], y_peer[k - 1]))
        return out

    def gathered(own, held, got, j):
        total = held[own, j].astype(F32)
        for k in range(3):
            total = total + got[k, j].astype(F32)
        return total

    def second_phase(p, copies):
        na, nb, _ = PIECES[p]
        _, _, a1s, a1r, b1s, b1r, a2s, a2r, b2s, b2r = bufs[p][:10]
        for copy in copies:
            copy.wait()
        for j in range(4):
            a2s[j] = gathered(mx, a1s, a1r, j).astype(BF16)
            total = gathered(my, b1s, b1r, j)
            for s in range(nb):
                value = total[s]
                if p == 2 and s == nb - 1:
                    value = two_terms(value)
                b2s[j, s] = value.astype(BF16)
        out = []
        for k in (2, 1, 3):
            out.append(send(a2s.at[(my + k) % 4], a2r.at[k - 1], y_peer[k - 1]))
            out.append(send(b2s.at[(mx + k) % 4], b2r.at[k - 1], x_peer[k - 1]))
        return out

    def third_phase(p, copies):
        na, nb, depth = PIECES[p]
        _, _, _, _, _, _, a2s, a2r, b2s, b2r, zs, zr = bufs[p]
        for copy in copies:
            copy.wait()
        for s in range(na + nb):
            own, held, got, j = (my, a2s, a2r, s) if s < na else (mx, b2s, b2r, s - na)
            total = gathered(own, held, got, j)
            for h in range(2):
                zs[pl.ds(2 * s + h, 8, stride=depth), :] = total[8 * h : 8 * h + 8]
        out = []
        for k in (4, 3, 5, 2, 6, 1, 7):
            start = pl.multiple_of(((mz + k) % 8) * depth, 8)
            out.append(send(zs.at[pl.ds(start, depth)], zr.at[k - 1], z_peer[k - 1]))
        return out

    def last_phase(p, copies, result):
        depth = PIECES[p][2]
        zs, zr = bufs[p][10:]
        for copy in copies:
            copy.wait()
        total = zs[pl.ds(pl.multiple_of(mz * depth, 8), depth), :]
        for k in range(7):
            total = total + zr[k]
        result[...] = total

    flight0 = core_phase(0)

    loads[5].wait()
    w = [[wmid_v[a, b] for b in range(3)] for a in range(3)]

    def back_of(start, count, a):
        total = None
        for b in range(3):
            term = dot_t1(m3[start : start + count, b * M : (b + 1) * M], w[a][b])
            total = term if total is None else total + term
        return total

    back[...] = back_of(WP, NP, 1)
    back[0 : NP - WP, :] += back_of(2 * WP, NP - WP, 0)
    back[WP:NP, :] += back_of(WP, NP - WP, 2)

    flight0 = first_phase(0, flight0)

    loads[4].wait()
    one_down.wait()
    one_up.wait()
    for r in range(BAND):
        h1x[(r + 1) * WP : (r + 2) * WP, :] = pad_rows(h1_v[r].astype(F32))
    h1x[0:WP, :] = pad_rows(jnp.where(rows > 0, h1up[...].astype(F32), 0.0))
    h1x[NP + WP : NP + 2 * WP, :] = pad_rows(jnp.where(rows < n_rows - 1, h1dn[...].astype(F32), 0.0))
    for a in range(3):
        grad = dot_t0(h1x[a * WP : a * WP + NP, :], m3[WP : WP + NP, :])
        for h in range(6):
            kf[6 * a + h] = grad[:, h * 128 : (h + 1) * 128].reshape(16, 16, 128)
    flight1 = core_phase(1)

    mid_down.wait()
    mid_up.wait()
    up = jnp.where(rows > 0, mup[...].astype(F32), 0.0)
    down = jnp.where(rows < n_rows - 1, mdn[...].astype(F32), 0.0)
    for value, start in ((up, 0), (down, NP + WP)):
        m3[start : start + WP, 0:M] = pltpu.roll(value, WP - 1, 0).astype(BF16)
        m3[start : start + WP, M : 2 * M] = value.astype(BF16)
        m3[start : start + WP, 2 * M : 3 * M] = pltpu.roll(value, 1, 0).astype(BF16)
    back[0:WP, :] += back_of(0, WP, 2)
    back[NP - WP : NP, :] += back_of(NP + WP, WP, 0)
    first[...] = jnp.where(h1x[WP : WP + NP, :].astype(F32) > 0, back[...], 0.0).astype(BF16)

    loads[6].wait()
    loads[7].wait()
    in_next.wait()
    in_prev.wait()
    for r in range(BAND):
        part = slice(r * WP, (r + 1) * WP)
        shifted[part, 0:E] = pad_rows(jnp.where(tm > 0, sprev[r].astype(F32), 0.0))
        shifted[part, E : 2 * E] = pad_rows(jnp.where(tm < n_tm - 1, snext[r].astype(F32), 0.0))
        shifted[part, 2 * E :] = pad_rows(inp_v[r, :, 2 * E :].astype(F32))
    grad = dot_t0(shifted[...], first[...])
    for h in range(2):
        d2[h] = grad[:, h * 128 : (h + 1) * 128].reshape(16, 64, 128)
    bh[0:8] = dot_t0(first[...], ones).reshape(8, 32, WP)
    flight2 = core_phase(2)

    prod_e[...] = dot_t1(first[...], win_v[0:E, :]).astype(BF16)
    early = send(prod_e, got_e, tm_prev)
    prod_l[...] = dot_t1(first[...], win_v[E : 2 * E, :]).astype(BF16)
    late = send(prod_l, got_l, tm_next)

    flight1 = first_phase(1, flight1)
    flight2 = first_phase(2, flight2)
    flight0 = second_phase(0, flight0)

    rest = og[:, 2 * E :].astype(F32) + dot_t1(first[...], win_v[2 * E :, :])
    for r in range(BAND):
        gi[r, :, 2 * E :] = rest[r * WP : r * WP + W].astype(BF16)
    early.wait()
    late.wait()
    for r in range(BAND):
        part = slice(r * WP, r * WP + WP)
        one = og[part, 0:E].astype(F32) + jnp.where(tm < n_tm - 1, got_e[part, :].astype(F32), 0.0)
        two = og[part, E : 2 * E].astype(F32) + jnp.where(tm > 0, got_l[part, :].astype(F32), 0.0)
        gi[r, :, 0:E] = one[:W].astype(BF16)
        gi[r, :, E : 2 * E] = two[:W].astype(BF16)
    store = pltpu.make_async_copy(gi, gi_out, load_sem.at[8])
    store.start()

    flight0 = third_phase(0, flight0)
    flight1 = second_phase(1, flight1)
    flight2 = second_phase(2, flight2)
    flight1 = third_phase(1, flight1)
    flight2 = third_phase(2, flight2)
    last_phase(0, flight0, f0_out)
    last_phase(1, flight1, f1_out)
    last_phase(2, flight2, f2_out)
    store.wait()


def scratch():
    def v(*shape, dtype=BF16):
        return pltpu.VMEM(shape, dtype)

    shapes = [
        v(BAND, W, C), v(BAND, W, M), v(BAND, W, M), v(BAND, W, C), v(BAND, W, C),
        v(C, M), v(3, 3, M, M), v(M, C),
        v(NP, C), v(NP, M), v(NP + 2 * WP, M), v(NP + 2 * WP, 3 * M), v(NP, C), v(NP, M),
        v(BAND, W, E), v(BAND, W, E), v(W, M), v(W, M), v(WP, M), v(WP, M), v(NP, M),
        v(NP, E), v(NP, E), v(NP, E), v(NP, E), v(BAND, W, C),
        v(NP, M, dtype=F32), v(2, 16, 64, 128, dtype=F32), v(18, 16, 16, 128, dtype=F32), v(2, 16, 64, 128, dtype=F32),
        v(16, 64, WP, dtype=F32), v(16, 32, WP, dtype=F32),
    ]
    for na, nb, depth in PIECES:
        tile = (16, 128)
        shapes += [v(4, 4, na + nb, *tile), v(4, 4, na + nb, *tile)]
        shapes += [v(4, 4, na, *tile), v(3, 4, na, *tile), v(4, 4, nb, *tile), v(3, 4, nb, *tile)]
        shapes += [v(4, na, *tile), v(3, na, *tile), v(4, nb, *tile), v(3, nb, *tile)]
        shapes += [v(8 * depth, 128, dtype=F32), v(7, depth, 128, dtype=F32)]
    shapes += [pltpu.SemaphoreType.DMA((9,)), pltpu.SemaphoreType.DMA((80,)), pltpu.SemaphoreType.DMA((80,))]
    return shapes


def finish(f0, f1, f2, d_in, d_mid, d_out, b_hidden, b_out):
    def lines(ref, start, count):
        return jnp.concatenate([ref[pl.ds(2 * start + h, count, stride=2), :] for h in range(2)], 1)

    d_in[...] = lines(f2, 0, 4)
    for a in range(3):
        d_mid[a] = lines(f1, 3 * a, 3)
    d_out[...] = lines(f0, 0, 4)
    bias = f2[8:9, :] + f2[9:10, :]
    b_hidden[...] = bias
    b_out[...] = bias


def on_device(inputs, hidden_one, hidden_two, outputs, cotangent, w_in, w_mid, w_out):
    anywhere = pl.BlockSpec(memory_space=pl.ANY)
    vmem = pl.BlockSpec(memory_space=pltpu.VMEM)
    gi, f0, f1, f2 = pl.pallas_call(
        kernel,
        out_shape=[
            jax.ShapeDtypeStruct((BAND, W, C), BF16),
            jax.ShapeDtypeStruct((PIECES[0][2], 128), F32),
            jax.ShapeDtypeStruct((PIECES[1][2], 128), F32),
            jax.ShapeDtypeStruct((PIECES[2][2], 128), F32),
        ],
        in_specs=[anywhere] * 8,
        out_specs=[anywhere, vmem, vmem, vmem],
        scratch_shapes=scratch(),
        compiler_params=pltpu.CompilerParams(
            collective_id=0, has_side_effects=True, vmem_limit_bytes=56 * 2**20
        ),
    )(inputs[0], hidden_one[0], hidden_two[0], outputs[0], cotangent[0], w_in, w_mid, w_out)
    d_in, d_mid, d_out, b_hidden, b_out = pl.pallas_call(
        finish,
        out_shape=[
            jax.ShapeDtypeStruct((4, M), F32),
            jax.ShapeDtypeStruct((3, 3, M), F32),
            jax.ShapeDtypeStruct((4, M), F32),
            jax.ShapeDtypeStruct((1, 128), F32),
            jax.ShapeDtypeStruct((1, 128), F32),
        ],
        in_specs=[vmem] * 3,
        out_specs=[vmem] * 5,
    )(f0, f1, f2)
    return gi[None], d_in, d_mid, d_out.T, b_hidden[0, 4:6], b_out[0, 0:4]


def solution(mesh):
    placed = (
        P("tm", "rows", None, None),
        P("tm", "rows", None, None),
        P("tm", "rows", None, None),
        P("tm", "rows", None, None),
        P("tm", "rows", None, None),
        P(),
        P(),
        P(),
    )
    return jax.shard_map(
        on_device,
        mesh=mesh,
        in_specs=placed,
        out_specs=(
            P("tm", "rows", None, None),
            P(("tm", "rows"), None),
            P(None, None, ("tm", "rows")),
            P(None, ("tm", "rows")),
            P(("tm", "rows")),
            P(("tm", "rows")),
        ),
        check_vma=False,
    )
```

```python
import jax
import jax.numpy as jnp
from jax import lax
from jax.experimental import pallas as pl
from jax.experimental.pallas import tpu as pltpu
from jax.sharding import PartitionSpec as P

F32 = jnp.float32
BF16 = jnp.bfloat16
MESH = pl.DeviceIdType.MESH

BAND = 4
W = 120
WP = 128
NP = BAND * WP
C = 1024
M = 256
E = C // 8
PIECES = ((4, 3, 16), (3, 3, 16), (5, 0, 16))


def dot_t0(a, b):
    return lax.dot_general(a, b, (((0,), (0,)), ((), ())), preferred_element_type=F32)


def dot_t1(a, b):
    return lax.dot_general(a, b, (((1,), (1,)), ((), ())), preferred_element_type=F32)


def pad_rows(value):
    return jnp.concatenate([value, jnp.zeros((WP - W, value.shape[1]), F32)], 0).astype(BF16)


def kernel(
    inp, h1, h2, outp, cot, w_in, w_mid, w_out,
    gi_out, f0_out, f1_out, f2_out,
    inp_v, h1_v, h2_v, outp_v, cot_v, win_v, wmid_v, wout_v,
    og, og_t, h2o, h1p, h1_t, m3, in_t, edge_t, first, mid_s, edge_mid, mup, mdn,
    prod_e, prod_l, got_e, got_l, gi, back, d0, kf, d2, bo, bh,
    cs0, cr0, a1s0, a1r0, b1s0, b1r0, a2s0, a2r0, b2s0, b2r0, zs0, zr0,
    cs1, cr1, a1s1, a1r1, b1s1, b1r1, a2s1, a2r1, b2s1, b2r1, zs1, zr1,
    cs2, cr2, xys2, xyr2, zs2, zr2,
    load_sem, send_sem, recv_sem,
):
    tm = lax.axis_index("tm")
    rows = lax.axis_index("rows")
    n_tm = lax.axis_size("tm")
    n_rows = lax.axis_size("rows")
    core = tm % 2
    mx = (tm // 2) % 4
    my = (tm // 8) * 2 + rows % 2
    mz = rows // 2

    def at(x, y, z, c):
        return (((y // 2) * 4 + x) * 2 + c, z * 2 + y % 2)

    sibling = at(mx, my, mz, 1 - core)
    xy_peer = {(i, j): at((mx + i) % 4, (my + j) % 4, mz, core) for i in range(4) for j in range(4) if i + j}
    x_peer = [xy_peer[k, 0] for k in range(1, 4)]
    y_peer = [xy_peer[0, k] for k in range(1, 4)]
    z_peer = [at(mx, my, (mz + k) % 8, core) for k in range(1, 8)]
    tm_next = ((tm + 1) % n_tm, rows)
    tm_prev = ((tm + n_tm - 1) % n_tm, rows)
    row_next = (tm, (rows + 1) % n_rows)
    row_prev = (tm, (rows + n_rows - 1) % n_rows)

    loads = []
    for i, (src, dst) in enumerate(
        ((outp, outp_v), (cot, cot_v), (w_out, wout_v), (h2, h2_v), (h1, h1_v), (inp, inp_v), (w_mid, wmid_v), (w_in, win_v))
    ):
        copy = pltpu.make_async_copy(src, dst, load_sem.at[i])
        copy.start()
        loads.append(copy)

    barrier = pltpu.get_barrier_semaphore()
    partners = [sibling, *xy_peer.values(), *z_peer, tm_next, tm_prev, row_next, row_prev]
    for peer in partners:
        pl.semaphore_signal(barrier, inc=1, device_id=peer, device_id_type=MESH)

    counter = [0]

    def send(src, dst, peer):
        i = counter[0]
        counter[0] += 1
        copy = pltpu.make_async_remote_copy(
            src_ref=src, dst_ref=dst, send_sem=send_sem.at[i], recv_sem=recv_sem.at[i],
            device_id=peer, device_id_type=MESH,
        )
        copy.start()
        return copy

    def dot(a, b):
        return jnp.dot(a, b, preferred_element_type=F32)

    def halves(held, value, *shape):
        for h in range(value.shape[1] // 128):
            held[h] = value[:, h * 128 : (h + 1) * 128].reshape(*shape, 128)

    def as_column(value):
        total = jnp.sum(value.astype(F32), 0, keepdims=True)
        return jnp.broadcast_to(total, (WP, M)).T.reshape(8, 32, WP)

    for copy in loads[:4]:
        copy.wait()
    for r in range(BAND):
        grad = jnp.where(outp_v[r].astype(F32) > 0, cot_v[r].astype(F32), 0.0)
        og[r * WP : (r + 1) * WP, :] = pad_rows(grad)
        h2o[r * WP : (r + 1) * WP, 0:M] = pad_rows(h2_v[r].astype(F32))
    h2o[:, M:] = jnp.ones((NP, WP), BF16)
    mid32 = jnp.where(h2o[:, 0:M].astype(F32) > 0, dot_t1(og[...], wout_v[...]), 0.0)
    mid = mid32.astype(BF16)
    mid_s[...] = mid
    edge_mid[0] = jnp.where(rows < n_rows - 1, mid32[NP - WP :], 0.0).astype(BF16)
    edge_mid[1] = jnp.where(rows > 0, mid32[:WP], 0.0).astype(BF16)
    m3[WP : WP + NP, 0:M] = pltpu.roll(mid32, NP - 1, 0).astype(BF16)
    m3[WP : WP + NP, M : 2 * M] = mid
    m3[WP : WP + NP, 2 * M : 3 * M] = pltpu.roll(mid32, 1, 0).astype(BF16)

    og_t[...] = og[...].T
    grad = dot(og_t[...], h2o[...])
    halves(d0, grad[:, 0:M], 16, 64)
    bo[...] = grad[:, M:].reshape(16, 64, WP)
    bh[8:16] = as_column(mid)
    loads[4].wait()
    for r in range(BAND):
        h1p[r * WP : (r + 1) * WP, :] = pad_rows(h1_v[r].astype(F32))
    h1_t[...] = h1p[...].T
    halves(kf.at[pl.ds(6, 6)], dot(h1_t[...], m3[WP : WP + NP, :]), 16, 16)
    loads[5].wait()
    for r in range(BAND):
        part = slice(r * WP, (r + 1) * WP)
        value = pad_rows(inp_v[r].astype(F32)).T
        edge_t[0, :, part] = jnp.where(tm < n_tm - 1, value[0:E].astype(F32), 0.0).astype(BF16)
        edge_t[1, :, part] = jnp.where(tm > 0, value[E : 2 * E].astype(F32), 0.0).astype(BF16)
        in_t[2 * E :, part] = value[2 * E :]

    pl.semaphore_wait(barrier, len(partners))
    mid_down = send(edge_mid.at[0], mup, row_next)
    mid_up = send(edge_mid.at[1], mdn, row_prev)
    in_next = send(edge_t.at[0], in_t.at[pl.ds(0, E)], tm_next)
    in_prev = send(edge_t.at[1], in_t.at[pl.ds(E, E)], tm_prev)

    def slab(piece, t, low, s):
        if piece == 0 and s >= 4 or piece == 1:
            tap = s - 1 if piece == 0 else s if s < 3 else s + 3
            parts = [kf[2 * tap + h, t, pl.ds(low, 8, stride=2), :] for h in range(2)]
        elif s < 4:
            held = d0 if piece == 0 else d2
            parts = [held[h, t, pl.ds(4 * low + s, 8, stride=8), :] for h in range(2)]
        else:
            lane = lax.broadcasted_iota(jnp.int32, (8, 128), 1)
            total = jnp.zeros((8, 128), F32)
            for j in range(4):
                total = jnp.where(lane == j, bo[t, pl.ds(4 * low + j, 8, stride=8), :], total)
            for j in range(2):
                total = jnp.where(lane == 4 + j, bh[t, pl.ds(2 * low + j, 8, stride=4), :], total)
            parts = [total, jnp.zeros((8, 128), F32)]
        return jnp.concatenate(parts, 0)

    def two_terms(value):
        total = value[0:8] + value[8:16]
        head = total.astype(BF16).astype(F32)
        return jnp.concatenate([head, total - head], 0)

    bufs = (
        (cs0, cr0, a1s0, a1r0, b1s0, b1r0, a2s0, a2r0, b2s0, b2r0, zs0, zr0),
        (cs1, cr1, a1s1, a1r1, b1s1, b1r1, a2s1, a2r1, b2s1, b2r1, zs1, zr1),
        (cs2, cr2, xys2, xyr2, None, None, None, None, None, None, zs2, zr2),
    )

    def core_phase(p):
        na, nb, _ = PIECES[p]
        cs, cr = bufs[p][:2]

        def body(x, carry):
            for y in range(4):
                t = ((y // 2) * 4 + x) * 2 + (1 - core)
                for s in range(na + nb):
                    value = slab(p, t, y % 2, s)
                    if p == 2 and s == 4:
                        value = two_terms(value)
                    cs[x, y, s] = value.astype(BF16)
            return carry

        lax.fori_loop(0, 4, body, 0)
        return [send(cs, cr, sibling)]

    def first_phase(p, copies):
        na, nb, _ = PIECES[p]
        cs, cr, a1s, a1r, b1s, b1r = bufs[p][:6]
        for copy in copies:
            copy.wait()

        def body(x, carry):
            for y in range(4):
                t = ((y // 2) * 4 + x) * 2 + core
                for s in range(na + nb):
                    value = slab(p, t, y % 2, s) + cr[x, y, s].astype(F32)
                    if p == 2 and s == 4:
                        value = two_terms(value)
                    if s < na:
                        a1s[x, y, s] = value.astype(BF16)
                    else:
                        b1s[y, x, s - na] = value.astype(BF16)
            return carry

        lax.fori_loop(0, 4, body, 0)
        out = []
        if p == 2:
            for (i, j), peer in sorted(xy_peer.items(), key=lambda item: -(item[0][0] % 3 + item[0][1] % 3)):
                out.append(send(a1s.at[(mx + i) % 4, (my + j) % 4], a1r.at[4 * i + j - 1], peer))
            return out
        for k in (2, 1, 3):
            out.append(send(a1s.at[(mx + k) % 4], a1r.at[k - 1], x_peer[k - 1]))
            out.append(send(b1s.at[(my + k) % 4], b1r.at[k - 1], y_peer[k - 1]))
        return out

    def gathered(own, held, got, j):
        total = held[own, j].astype(F32)
        for k in range(3):
            total = total + got[k, j].astype(F32)
        return total

    def second_phase(p, copies):
        na, nb, _ = PIECES[p]
        _, _, a1s, a1r, b1s, b1r, a2s, a2r, b2s, b2r = bufs[p][:10]
        for copy in copies:
            copy.wait()
        for j in range(4):
            a2s[j] = gathered(mx, a1s, a1r, j).astype(BF16)
            b2s[j] = gathered(my, b1s, b1r, j).astype(BF16)
        out = []
        for k in (2, 1, 3):
            out.append(send(a2s.at[(my + k) % 4], a2r.at[k - 1], y_peer[k - 1]))
            out.append(send(b2s.at[(mx + k) % 4], b2r.at[k - 1], x_peer[k - 1]))
        return out

    def third_phase(p, copies):
        na, nb, depth = PIECES[p]
        _, _, xys, xyr, _, _, a2s, a2r, b2s, b2r, zs, zr = bufs[p]
        for copy in copies:
            copy.wait()
        for s in range(na + nb):
            if p == 2:
                total = xys[mx, my, s].astype(F32)
                for k in range(15):
                    total = total + xyr[k, s].astype(F32)
            else:
                own, held, got, j = (my, a2s, a2r, s) if s < na else (mx, b2s, b2r, s - na)
                total = gathered(own, held, got, j)
            for h in range(2):
                zs[pl.ds(2 * s + h, 8, stride=depth), :] = total[8 * h : 8 * h + 8]
        out = []
        for k in (4, 3, 5, 2, 6, 1, 7):
            start = pl.multiple_of(((mz + k) % 8) * depth, 8)
            out.append(send(zs.at[pl.ds(start, depth)], zr.at[k - 1], z_peer[k - 1]))
        return out

    def last_phase(p, copies, result):
        depth = PIECES[p][2]
        zs, zr = bufs[p][10:]
        for copy in copies:
            copy.wait()
        total = zs[pl.ds(pl.multiple_of(mz * depth, 8), depth), :]
        for k in range(7):
            total = total + zr[k]
        result[...] = total

    flight0 = core_phase(0)

    def back_of(start, count, a):
        total = None
        for b in range(3):
            term = dot_t1(m3[start : start + count, b * M : (b + 1) * M], wmid_v[a, b])
            total = term if total is None else total + term
        return total

    loads[6].wait()
    back[...] = back_of(WP, NP, 1)
    back[0 : NP - WP, :] += back_of(2 * WP, NP - WP, 0)
    back[WP:NP, :] += back_of(WP, NP - WP, 2)

    flight0 = first_phase(0, flight0)

    mid_down.wait()
    mid_up.wait()
    for held, start in ((mup, 0), (mdn, NP + WP)):
        value = held[...].astype(F32)
        m3[start : start + WP, 0:M] = pltpu.roll(value, WP - 1, 0).astype(BF16)
        m3[start : start + WP, M : 2 * M] = held[...]
        m3[start : start + WP, 2 * M : 3 * M] = pltpu.roll(value, 1, 0).astype(BF16)
    halves(kf.at[pl.ds(0, 6)], dot(h1_t[...], m3[2 * WP : 2 * WP + NP, :]), 16, 16)
    halves(kf.at[pl.ds(12, 6)], dot(h1_t[...], m3[0:NP, :]), 16, 16)
    flight1 = core_phase(1)

    back[0:WP, :] += back_of(0, WP, 2)
    back[NP - WP : NP, :] += back_of(NP + WP, WP, 0)
    first_grad = jnp.where(h1p[...].astype(F32) > 0, back[...], 0.0).astype(BF16)
    first[...] = first_grad
    bh[0:8] = as_column(first_grad)
    in_next.wait()
    in_prev.wait()
    halves(d2, dot(in_t[...], first[...]), 16, 64)
    flight2 = core_phase(2)
    flight1 = first_phase(1, flight1)
    flight2 = first_phase(2, flight2)

    loads[7].wait()
    edge = dot_t1(first[...], win_v[0 : 2 * E, :])
    prod_e[...] = jnp.where(tm > 0, edge[:, 0:E], 0.0).astype(BF16)
    prod_l[...] = jnp.where(tm < n_tm - 1, edge[:, E:], 0.0).astype(BF16)
    early = send(prod_e, got_e, tm_prev)
    late = send(prod_l, got_l, tm_next)

    flight0 = second_phase(0, flight0)

    rest = og[:, 2 * E :].astype(F32) + dot_t1(first[...], win_v[2 * E :, :])
    for r in range(BAND):
        gi[r, :, 2 * E :] = rest[r * WP : r * WP + W].astype(BF16)
    flight1 = second_phase(1, flight1)
    flight0 = third_phase(0, flight0)
    early.wait()
    late.wait()
    for r in range(BAND):
        part = slice(r * WP, r * WP + WP)
        one = og[part, 0:E].astype(F32) + got_e[part, :].astype(F32)
        two = og[part, E : 2 * E].astype(F32) + got_l[part, :].astype(F32)
        gi[r, :, 0:E] = one[:W].astype(BF16)
        gi[r, :, E : 2 * E] = two[:W].astype(BF16)
    store = pltpu.make_async_copy(gi, gi_out, load_sem.at[8])
    store.start()

    flight1 = third_phase(1, flight1)
    flight2 = third_phase(2, flight2)
    last_phase(0, flight0, f0_out)
    last_phase(1, flight1, f1_out)
    last_phase(2, flight2, f2_out)
    store.wait()


def scratch():
    def v(*shape, dtype=BF16):
        return pltpu.VMEM(shape, dtype)

    shapes = [
        v(BAND, W, C), v(BAND, W, M), v(BAND, W, M), v(BAND, W, C), v(BAND, W, C),
        v(C, M), v(3, 3, M, M), v(M, C),
        v(NP, C), v(C, NP), v(NP, M + WP), v(NP, M), v(M, NP), v(NP + 2 * WP, 3 * M),
        v(C, NP), v(2, E, NP), v(NP, M), v(NP, M), v(2, WP, M), v(WP, M), v(WP, M),
        v(NP, E), v(NP, E), v(NP, E), v(NP, E), v(BAND, W, C),
        v(NP, M, dtype=F32), v(2, 16, 64, 128, dtype=F32), v(18, 16, 16, 128, dtype=F32), v(2, 16, 64, 128, dtype=F32),
        v(16, 64, WP, dtype=F32), v(16, 32, WP, dtype=F32),
    ]
    tile = (16, 128)
    for na, nb, depth in PIECES:
        shapes += [v(4, 4, na + nb, *tile), v(4, 4, na + nb, *tile)]
        if nb:
            shapes += [v(4, 4, na, *tile), v(3, 4, na, *tile), v(4, 4, nb, *tile), v(3, 4, nb, *tile)]
            shapes += [v(4, na, *tile), v(3, na, *tile), v(4, nb, *tile), v(3, nb, *tile)]
        else:
            shapes += [v(4, 4, na, *tile), v(15, na, *tile)]
        shapes += [v(8 * depth, 128, dtype=F32), v(7, depth, 128, dtype=F32)]
    shapes += [pltpu.SemaphoreType.DMA((9,)), pltpu.SemaphoreType.DMA((80,)), pltpu.SemaphoreType.DMA((80,))]
    return shapes


def finish(
    gi_in, f0_in, f1_in, f2_in, gi, d_in, d_mid, d_out, b_hidden, b_out,
    held, f0, f1, f2, d_in_v, d_mid_v, d_out_v, b_hidden_v, b_out_v, load_sem, store_sem,
):
    small = [(f0_in, f0), (f1_in, f1), (f2_in, f2)]
    large = [(gi_in.at[r], held.at[r]) for r in range(BAND)]
    loads = [pltpu.make_async_copy(src, dst, load_sem.at[i]) for i, (src, dst) in enumerate(large + small)]
    for load in loads:
        load.start()
    results = [(d_in_v, d_in), (d_mid_v, d_mid), (d_out_v, d_out), (b_hidden_v, b_hidden), (b_out_v, b_out)]
    results = [(held.at[r], gi.at[r]) for r in range(BAND)] + results
    stores = [pltpu.make_async_copy(src, dst, store_sem.at[i]) for i, (src, dst) in enumerate(results)]

    def lines(ref, start, count):
        return jnp.concatenate([ref[pl.ds(2 * start + h, count, stride=2), :] for h in range(2)], 1)

    for load in loads[BAND:]:
        load.wait()
    d_in_v[...] = lines(f2, 0, 4)
    d_mid_v[0] = lines(f1, 0, 3)
    d_mid_v[1] = lines(f0, 4, 3)
    d_mid_v[2] = lines(f1, 3, 3)
    d_out_v[...] = lines(f0, 0, 4)
    bias = f2[8, :] + f2[9, :]
    b_hidden_v[...] = bias[4:6]
    b_out_v[...] = bias[0:4]
    for store in stores[BAND:]:
        store.start()
    for load, store in zip(loads[:BAND], stores[:BAND]):
        load.wait()
        store.start()
    for store in stores:
        store.wait()


def on_device(inputs, hidden_one, hidden_two, outputs, cotangent, w_in, w_mid, w_out):
    anywhere = pl.BlockSpec(memory_space=pl.ANY)
    vmem = pl.BlockSpec(memory_space=pltpu.VMEM)
    gi, f0, f1, f2 = pl.pallas_call(
        kernel,
        out_shape=[
            jax.ShapeDtypeStruct((BAND, W, C), BF16),
            jax.ShapeDtypeStruct((PIECES[0][2], 128), F32),
            jax.ShapeDtypeStruct((PIECES[1][2], 128), F32),
            jax.ShapeDtypeStruct((PIECES[2][2], 128), F32),
        ],
        in_specs=[anywhere] * 8,
        out_specs=[anywhere, vmem, vmem, vmem],
        scratch_shapes=scratch(),
        compiler_params=pltpu.CompilerParams(
            collective_id=0, has_side_effects=True, vmem_limit_bytes=56 * 2**20
        ),
    )(inputs[0], hidden_one[0], hidden_two[0], outputs[0], cotangent[0], w_in, w_mid, w_out)
    gi, d_in, d_mid, d_out, b_hidden, b_out = pl.pallas_call(
        finish,
        out_shape=[
            jax.ShapeDtypeStruct((BAND, W, C), BF16),
            jax.ShapeDtypeStruct((4, M), F32),
            jax.ShapeDtypeStruct((3, 3, M), F32),
            jax.ShapeDtypeStruct((4, M), F32),
            jax.ShapeDtypeStruct((2,), F32),
            jax.ShapeDtypeStruct((4,), F32),
        ],
        in_specs=[anywhere] * 4,
        out_specs=[anywhere] * 6,
        scratch_shapes=[
            pltpu.VMEM((BAND, W, C), BF16),
            pltpu.VMEM((PIECES[0][2], 128), F32),
            pltpu.VMEM((PIECES[1][2], 128), F32),
            pltpu.VMEM((PIECES[2][2], 128), F32),
            pltpu.VMEM((4, M), F32),
            pltpu.VMEM((3, 3, M), F32),
            pltpu.VMEM((4, M), F32),
            pltpu.VMEM((2,), F32),
            pltpu.VMEM((4,), F32),
            pltpu.SemaphoreType.DMA((BAND + 3,)),
            pltpu.SemaphoreType.DMA((BAND + 5,)),
        ],
    )(gi, f0, f1, f2)
    return gi[None], d_in, d_mid, d_out.T, b_hidden, b_out


def solution(mesh):
    placed = (
        P("tm", "rows", None, None),
        P("tm", "rows", None, None),
        P("tm", "rows", None, None),
        P("tm", "rows", None, None),
        P("tm", "rows", None, None),
        P(),
        P(),
        P(),
    )
    return jax.shard_map(
        on_device,
        mesh=mesh,
        in_specs=placed,
        out_specs=(
            P("tm", "rows", None, None),
            P(("tm", "rows"), None),
            P(None, None, ("tm", "rows")),
            P(None, ("tm", "rows")),
            P(("tm", "rows")),
            P(("tm", "rows")),
        ),
        check_vma=False,
    )
```

```python
import jax
import jax.numpy as jnp
from jax import lax
from jax.experimental import pallas as pl
from jax.experimental.pallas import tpu as pltpu
from jax.sharding import PartitionSpec as P

F32 = jnp.float32
BF16 = jnp.bfloat16
MESH = pl.DeviceIdType.MESH

BAND = 4
W = 120
WP = 128
NP = BAND * WP
C = 1024
M = 256
E = C // 8
PIECES = ((4, 3), (3, 3), (5, 0))
DEPTH = 16


def dot_t0(a, b):
    return lax.dot_general(a, b, (((0,), (0,)), ((), ())), preferred_element_type=F32)


def dot_t1(a, b):
    return lax.dot_general(a, b, (((1,), (1,)), ((), ())), preferred_element_type=F32)


def pad_rows(value):
    return jnp.concatenate([value, jnp.zeros((WP - W, value.shape[1]), F32)], 0).astype(BF16)


def kernel(
    inp, h1, h2, outp, cot, w_in, w_mid, w_out,
    gi_out, f0_out, f1_out, f2_out, f3_out,
    inp_v, h1_v, h2_v, outp_v, cot_v, win_v, wmid_v, wout_v,
    og, og_t, h2o, h1p, h1_t, m3, in_t, edge_t, first, mid_s, edge_mid, mup, mdn,
    prod_e, prod_l, got_e, got_l, gi, back, d0, kf, d2, bo, bh,
    cs0, cr0, a1s0, a1r0, b1s0, b1r0, a2s0, a2r0, b2s0, b2r0, zf0, zs0, zr0,
    cs1, cr1, a1s1, a1r1, b1s1, b1r1, a2s1, a2r1, b2s1, b2r1, zf1, zs1, zr1,
    cs2, cr2, xys2, xyr2, zf2, zs2, zr2, zf3, zs3, zr3, sum3, xys3, xyr3,
    load_sem, send_sem, recv_sem,
):
    tm = lax.axis_index("tm")
    rows = lax.axis_index("rows")
    n_tm = lax.axis_size("tm")
    n_rows = lax.axis_size("rows")
    core = tm % 2
    mx = (tm // 2) % 4
    my = (tm // 8) * 2 + rows % 2
    mz = rows // 2

    def at(x, y, z, c):
        return (((y // 2) * 4 + x) * 2 + c, z * 2 + y % 2)

    sibling = at(mx, my, mz, 1 - core)
    xy_peer = {(i, j): at((mx + i) % 4, (my + j) % 4, mz, core) for i in range(4) for j in range(4) if i + j}
    x_peer = [xy_peer[k, 0] for k in range(1, 4)]
    y_peer = [xy_peer[0, k] for k in range(1, 4)]
    z_peer = [at(mx, my, (mz + k) % 8, core) for k in range(1, 8)]
    tm_next = ((tm + 1) % n_tm, rows)
    tm_prev = ((tm + n_tm - 1) % n_tm, rows)
    row_next = (tm, (rows + 1) % n_rows)
    row_prev = (tm, (rows + n_rows - 1) % n_rows)

    loads = []
    for i, (src, dst) in enumerate(
        ((outp, outp_v), (cot, cot_v), (w_out, wout_v), (h2, h2_v), (h1, h1_v), (inp, inp_v), (w_mid, wmid_v), (w_in, win_v))
    ):
        copy = pltpu.make_async_copy(src, dst, load_sem.at[i])
        copy.start()
        loads.append(copy)

    barrier = pltpu.get_barrier_semaphore()
    partners = [sibling, *xy_peer.values(), *z_peer, tm_next, tm_prev, row_next, row_prev]
    for peer in partners:
        pl.semaphore_signal(barrier, inc=1, device_id=peer, device_id_type=MESH)

    counter = [0]

    def send(src, dst, peer):
        i = counter[0]
        counter[0] += 1
        copy = pltpu.make_async_remote_copy(
            src_ref=src, dst_ref=dst, send_sem=send_sem.at[i], recv_sem=recv_sem.at[i],
            device_id=peer, device_id_type=MESH,
        )
        copy.start()
        return copy

    def dot(a, b):
        return jnp.dot(a, b, preferred_element_type=F32)

    def halves(held, value, *shape):
        for h in range(value.shape[1] // 128):
            held[h] = value[:, h * 128 : (h + 1) * 128].reshape(*shape, 128)

    def as_column(value):
        total = jnp.sum(value.astype(F32), 0, keepdims=True)
        return jnp.broadcast_to(total, (WP, M)).T.reshape(8, 32, WP)

    for copy in loads[:4]:
        copy.wait()
    for r in range(BAND):
        grad = jnp.where(outp_v[r].astype(F32) > 0, cot_v[r].astype(F32), 0.0)
        og[r * WP : (r + 1) * WP, :] = pad_rows(grad)
        h2o[r * WP : (r + 1) * WP, 0:M] = pad_rows(h2_v[r].astype(F32))
    h2o[:, M:] = jnp.ones((NP, WP), BF16)
    mid32 = jnp.where(h2o[:, 0:M].astype(F32) > 0, dot_t1(og[...], wout_v[...]), 0.0)
    mid = mid32.astype(BF16)
    mid_s[...] = mid
    edge_mid[0] = jnp.where(rows < n_rows - 1, mid32[NP - WP :], 0.0).astype(BF16)
    edge_mid[1] = jnp.where(rows > 0, mid32[:WP], 0.0).astype(BF16)
    m3[WP : WP + NP, 0:M] = pltpu.roll(mid32, NP - 1, 0).astype(BF16)
    m3[WP : WP + NP, M : 2 * M] = mid
    m3[WP : WP + NP, 2 * M : 3 * M] = pltpu.roll(mid32, 1, 0).astype(BF16)

    og_t[...] = og[...].T
    grad = dot(og_t[...], h2o[...])
    halves(d0, grad[:, 0:M], 16, 64)
    bo[...] = grad[:, M:].reshape(16, 64, WP)
    bh[8:16] = as_column(mid)
    loads[4].wait()
    for r in range(BAND):
        h1p[r * WP : (r + 1) * WP, :] = pad_rows(h1_v[r].astype(F32))
    h1_t[...] = h1p[...].T
    halves(kf.at[pl.ds(6, 6)], dot(h1_t[...], m3[WP : WP + NP, :]), 16, 16)
    loads[5].wait()
    for r in range(BAND):
        part = slice(r * WP, (r + 1) * WP)
        value = pad_rows(inp_v[r].astype(F32)).T
        edge_t[0, :, part] = jnp.where(tm < n_tm - 1, value[0:E].astype(F32), 0.0).astype(BF16)
        edge_t[1, :, part] = jnp.where(tm > 0, value[E : 2 * E].astype(F32), 0.0).astype(BF16)
        in_t[2 * E :, part] = value[2 * E :]

    pl.semaphore_wait(barrier, len(partners))
    mid_down = send(edge_mid.at[0], mup, row_next)
    mid_up = send(edge_mid.at[1], mdn, row_prev)
    in_next = send(edge_t.at[0], in_t.at[pl.ds(0, E)], tm_next)
    in_prev = send(edge_t.at[1], in_t.at[pl.ds(E, E)], tm_prev)

    def slab(piece, t, low, s):
        if piece == 0 and s >= 4 or piece == 1:
            tap = s - 1 if piece == 0 else s if s < 3 else s + 3
            parts = [kf[2 * tap + h, t, pl.ds(low, 8, stride=2), :] for h in range(2)]
        elif piece == 0 or s != 2:
            held, j = (d0, s) if piece == 0 else (d2, s - s // 3)
            parts = [held[h, t, pl.ds(4 * low + j, 8, stride=8), :] for h in range(2)]
        else:
            lane = lax.broadcasted_iota(jnp.int32, (8, 128), 1)
            total = jnp.zeros((8, 128), F32)
            for j in range(4):
                total = jnp.where(lane == j, bo[t, pl.ds(4 * low + j, 8, stride=8), :], total)
            for j in range(2):
                total = jnp.where(lane == 4 + j, bh[t, pl.ds(2 * low + j, 8, stride=4), :], total)
            parts = [total, jnp.zeros((8, 128), F32)]
        return jnp.concatenate(parts, 0)

    def two_terms(value):
        total = value[0:8] + value[8:16]
        head = total.astype(BF16).astype(F32)
        return jnp.concatenate([head, total - head], 0)

    bufs = (
        (cs0, cr0, a1s0, a1r0, b1s0, b1r0, a2s0, a2r0, b2s0, b2r0, zf0, zs0, zr0),
        (cs1, cr1, a1s1, a1r1, b1s1, b1r1, a2s1, a2r1, b2s1, b2r1, zf1, zs1, zr1),
        (cs2, cr2, xys2, xyr2, None, None, None, None, None, None, zf2, zs2, zr2),
    )

    late3 = []

    def core_phase(p):
        na, nb = PIECES[p]
        cs, cr = bufs[p][:2]

        def body(x, carry):
            for y in range(4):
                t = ((y // 2) * 4 + x) * 2 + (1 - core)
                for s in range(na + nb):
                    value = slab(p, t, y % 2, s)
                    if p == 2 and s == 2:
                        value = two_terms(value)
                    cs[x, y, s] = value.astype(BF16)
            return carry

        lax.fori_loop(0, 4, body, 0)
        return [send(cs, cr, sibling)]

    def first_phase(p, copies):
        na, nb = PIECES[p]
        cs, cr, a1s, a1r, b1s, b1r = bufs[p][:6]
        for copy in copies:
            copy.wait()

        def body(x, carry):
            for y in range(4):
                t = ((y // 2) * 4 + x) * 2 + core
                for s in range(na + nb):
                    value = slab(p, t, y % 2, s) + cr[x, y, s].astype(F32)
                    if p == 2 and s == 2:
                        value = two_terms(value)
                    if p == 2 and s > 2:
                        for h in range(2):
                            row = x * 16 + y * 4 + 2 * (s - 3) + h
                            zf3[pl.ds(row, 8, stride=64), :] = value[8 * h : 8 * h + 8]
                    elif s < na:
                        a1s[x, y, s] = value.astype(BF16)
                    else:
                        b1s[y, x, s - na] = value.astype(BF16)
            return carry

        lax.fori_loop(0, 4, body, 0)
        out = []
        if p == 2:
            zs3[...] = zf3[...].reshape(8, 64, 128).astype(BF16)
            for k in (4, 3, 5, 2, 6, 1, 7):
                late3.append(send(zs3.at[(mz + k) % 8], zr3.at[k - 1], z_peer[k - 1]))
            for (i, j), peer in sorted(xy_peer.items(), key=lambda item: -(item[0][0] % 3 + item[0][1] % 3)):
                out.append(send(a1s.at[(mx + i) % 4, (my + j) % 4], a1r.at[4 * i + j - 1], peer))
            return out
        for k in (2, 1, 3):
            out.append(send(a1s.at[(mx + k) % 4], a1r.at[k - 1], x_peer[k - 1]))
            out.append(send(b1s.at[(my + k) % 4], b1r.at[k - 1], y_peer[k - 1]))
        return out

    def gathered(own, held, got, j):
        total = held[own, j].astype(F32)
        for k in range(3):
            total = total + got[k, j].astype(F32)
        return total

    def second_phase(p, copies):
        na, nb = PIECES[p]
        _, _, a1s, a1r, b1s, b1r, a2s, a2r, b2s, b2r = bufs[p][:10]
        for copy in copies:
            copy.wait()
        for j in range(4):
            a2s[j] = gathered(mx, a1s, a1r, j).astype(BF16)
            b2s[j] = gathered(my, b1s, b1r, j).astype(BF16)
        out = []
        for k in (2, 1, 3):
            out.append(send(a2s.at[(my + k) % 4], a2r.at[k - 1], y_peer[k - 1]))
            out.append(send(b2s.at[(mx + k) % 4], b2r.at[k - 1], x_peer[k - 1]))
        return out

    def third_phase(p, copies):
        na, nb = PIECES[p]
        _, _, xys, xyr, _, _, a2s, a2r, b2s, b2r, zf, zs, zr = bufs[p]
        for copy in copies:
            copy.wait()
        for s in range(3 if p == 2 else na + nb):
            if p == 2:
                total = xys[mx, my, s].astype(F32)
                for k in range(15):
                    total = total + xyr[k, s].astype(F32)
                if s == 2:
                    total = two_terms(total)
            else:
                own, held, got, j = (my, a2s, a2r, s) if s < na else (mx, b2s, b2r, s - na)
                total = gathered(own, held, got, j)
            for h in range(2):
                zf[pl.ds(2 * s + h, 8, stride=DEPTH), :] = total[8 * h : 8 * h + 8]
        zs[...] = zf[...].reshape(8, DEPTH, 128).astype(BF16)
        return [send(zs.at[(mz + k) % 8], zr.at[k - 1], z_peer[k - 1]) for k in (4, 3, 5, 2, 6, 1, 7)]

    def last_phase(p, copies, result):
        zf, _, zr = bufs[p][10:]
        for copy in copies:
            copy.wait()
        total = zf[pl.ds(pl.multiple_of(mz * DEPTH, 8), DEPTH), :]
        for k in range(7):
            total = total + zr[k].astype(F32)
        result[...] = total

    def cross_phase(copies):
        for copy in copies:
            copy.wait()
        total = zs3[mz].astype(F32)
        for k in range(7):
            total = total + zr3[k].astype(F32)
        sum3[0:64, :] = total
        for i in range(16):
            xys3[i] = sum3[4 * i : 4 * i + 8, :]
        out = []
        for (i, j), peer in sorted(xy_peer.items(), key=lambda item: -(item[0][0] % 3 + item[0][1] % 3)):
            out.append(send(xys3.at[((mx + i) % 4) * 4 + (my + j) % 4], xyr3.at[4 * i + j - 1], peer))
        return out

    def cross_end(copies, result):
        for copy in copies:
            copy.wait()
        total = xys3[mx * 4 + my]
        for k in range(15):
            total = total + xyr3[k]
        result[...] = total

    flight0 = core_phase(0)

    def back_of(start, count, a):
        total = None
        for b in range(3):
            term = dot_t1(m3[start : start + count, b * M : (b + 1) * M], wmid_v[a, b])
            total = term if total is None else total + term
        return total

    loads[6].wait()
    back[...] = back_of(WP, NP, 1)
    back[0 : NP - WP, :] += back_of(2 * WP, NP - WP, 0)
    back[WP:NP, :] += back_of(WP, NP - WP, 2)

    flight0 = first_phase(0, flight0)
    halves(kf.at[pl.ds(0, 6)], dot(h1_t[:, 0 : NP - WP], m3[2 * WP : WP + NP, :]), 16, 16)
    halves(kf.at[pl.ds(12, 6)], dot(h1_t[:, WP:NP], m3[WP:NP, :]), 16, 16)

    mid_down.wait()
    mid_up.wait()
    for held, start in ((mup, 0), (mdn, NP + WP)):
        value = held[...].astype(F32)
        m3[start : start + WP, 0:M] = pltpu.roll(value, WP - 1, 0).astype(BF16)
        m3[start : start + WP, M : 2 * M] = held[...]
        m3[start : start + WP, 2 * M : 3 * M] = pltpu.roll(value, 1, 0).astype(BF16)
    for first_tap, grad in (
        (0, dot(h1_t[:, NP - WP :], m3[NP + WP :, :])),
        (12, dot(h1_t[:, 0:WP], m3[0:WP, :])),
    ):
        for h in range(6):
            kf[first_tap + h] += grad[:, h * 128 : (h + 1) * 128].reshape(16, 16, 128)
    flight1 = core_phase(1)

    back[0:WP, :] += back_of(0, WP, 2)
    back[NP - WP : NP, :] += back_of(NP + WP, WP, 0)
    first_grad = jnp.where(h1p[...].astype(F32) > 0, back[...], 0.0).astype(BF16)
    first[...] = first_grad
    flight1 = first_phase(1, flight1)
    bh[0:8] = as_column(first_grad)
    in_next.wait()
    in_prev.wait()
    halves(d2, dot(in_t[...], first[...]), 16, 64)
    flight2 = core_phase(2)

    loads[7].wait()
    edge = dot_t1(first[...], win_v[0 : 2 * E, :])
    prod_e[...] = jnp.where(tm > 0, edge[:, 0:E], 0.0).astype(BF16)
    prod_l[...] = jnp.where(tm < n_tm - 1, edge[:, E:], 0.0).astype(BF16)
    early = send(prod_e, got_e, tm_prev)
    late = send(prod_l, got_l, tm_next)
    flight2 = first_phase(2, flight2)

    rest = og[:, 2 * E :].astype(F32) + dot_t1(first[...], win_v[2 * E :, :])
    for r in range(BAND):
        gi[r, :, 2 * E :] = rest[r * WP : r * WP + W].astype(BF16)
    flight0 = second_phase(0, flight0)
    flight1 = second_phase(1, flight1)
    flight0 = third_phase(0, flight0)
    early.wait()
    late.wait()
    for r in range(BAND):
        part = slice(r * WP, r * WP + WP)
        one = og[part, 0:E].astype(F32) + got_e[part, :].astype(F32)
        two = og[part, E : 2 * E].astype(F32) + got_l[part, :].astype(F32)
        gi[r, :, 0:E] = one[:W].astype(BF16)
        gi[r, :, E : 2 * E] = two[:W].astype(BF16)
    store = pltpu.make_async_copy(gi, gi_out, load_sem.at[8])
    store.start()

    flight2 = third_phase(2, flight2)
    flight3 = cross_phase(late3)
    flight1 = third_phase(1, flight1)
    last_phase(0, flight0, f0_out)
    last_phase(2, flight2, f2_out)
    cross_end(flight3, f3_out)
    last_phase(1, flight1, f1_out)
    store.wait()


def scratch():
    def v(*shape, dtype=BF16):
        return pltpu.VMEM(shape, dtype)

    shapes = [
        v(BAND, W, C), v(BAND, W, M), v(BAND, W, M), v(BAND, W, C), v(BAND, W, C),
        v(C, M), v(3, 3, M, M), v(M, C),
        v(NP, C), v(C, NP), v(NP, M + WP), v(NP, M), v(M, NP), v(NP + 2 * WP, 3 * M),
        v(C, NP), v(2, E, NP), v(NP, M), v(NP, M), v(2, WP, M), v(WP, M), v(WP, M),
        v(NP, E), v(NP, E), v(NP, E), v(NP, E), v(BAND, W, C),
        v(NP, M, dtype=F32), v(2, 16, 64, 128, dtype=F32), v(18, 16, 16, 128, dtype=F32), v(2, 16, 64, 128, dtype=F32),
        v(16, 64, WP, dtype=F32), v(16, 32, WP, dtype=F32),
    ]
    tile = (16, 128)
    for na, nb in PIECES:
        shapes += [v(4, 4, na + nb, *tile), v(4, 4, na + nb, *tile)]
        if nb:
            shapes += [v(4, 4, na, *tile), v(3, 4, na, *tile), v(4, 4, nb, *tile), v(3, 4, nb, *tile)]
            shapes += [v(4, na, *tile), v(3, na, *tile), v(4, nb, *tile), v(3, nb, *tile)]
        else:
            shapes += [v(4, 4, 3, *tile), v(15, 3, *tile)]
        shapes += [v(8 * DEPTH, 128, dtype=F32), v(8, DEPTH, 128), v(7, DEPTH, 128)]
    shapes += [v(8 * 64, 128, dtype=F32), v(8, 64, 128), v(7, 64, 128)]
    shapes += [v(72, 128, dtype=F32), v(16, 8, 128, dtype=F32), v(15, 8, 128, dtype=F32)]
    shapes += [pltpu.SemaphoreType.DMA((9,)), pltpu.SemaphoreType.DMA((100,)), pltpu.SemaphoreType.DMA((100,))]
    return shapes


def finish(
    gi_in, f0_in, f1_in, f2_in, f3_in, gi, d_in, d_mid, d_out, b_hidden, b_out,
    held, f0, f1, f2, f3, d_in_v, d_mid_v, d_out_v, b_hidden_v, b_out_v, load_sem, store_sem,
):
    small = [(f0_in, f0), (f1_in, f1), (f2_in, f2), (f3_in, f3)]
    large = [(gi_in.at[r], held.at[r]) for r in range(BAND)]
    loads = [pltpu.make_async_copy(src, dst, load_sem.at[i]) for i, (src, dst) in enumerate(large + small)]
    for load in loads:
        load.start()
    results = [(d_in_v, d_in), (d_mid_v, d_mid), (d_out_v, d_out), (b_hidden_v, b_hidden), (b_out_v, b_out)]
    results = [(held.at[r], gi.at[r]) for r in range(BAND)] + results
    stores = [pltpu.make_async_copy(src, dst, store_sem.at[i]) for i, (src, dst) in enumerate(results)]

    def lines(ref, start, count):
        return jnp.concatenate([ref[pl.ds(2 * start + h, count, stride=2), :] for h in range(2)], 1)

    for load in loads[BAND:]:
        load.wait()
    d_in_v[0:2, :] = lines(f2, 0, 2)
    d_in_v[2:4, :] = lines(f3, 0, 2)
    d_mid_v[0] = lines(f1, 0, 3)
    d_mid_v[1] = lines(f0, 4, 3)
    d_mid_v[2] = lines(f1, 3, 3)
    d_out_v[...] = lines(f0, 0, 4)
    bias = f2[4, :] + f2[5, :]
    b_hidden_v[...] = bias[4:6]
    b_out_v[...] = bias[0:4]
    for store in stores[BAND:]:
        store.start()
    for load, store in zip(loads[:BAND], stores[:BAND]):
        load.wait()
        store.start()
    for store in stores:
        store.wait()


def on_device(inputs, hidden_one, hidden_two, outputs, cotangent, w_in, w_mid, w_out):
    anywhere = pl.BlockSpec(memory_space=pl.ANY)
    vmem = pl.BlockSpec(memory_space=pltpu.VMEM)
    gi, f0, f1, f2, f3 = pl.pallas_call(
        kernel,
        out_shape=[
            jax.ShapeDtypeStruct((BAND, W, C), BF16),
            jax.ShapeDtypeStruct((DEPTH, 128), F32),
            jax.ShapeDtypeStruct((DEPTH, 128), F32),
            jax.ShapeDtypeStruct((DEPTH, 128), F32),
            jax.ShapeDtypeStruct((8, 128), F32),
        ],
        in_specs=[anywhere] * 8,
        out_specs=[anywhere, vmem, vmem, vmem, vmem],
        scratch_shapes=scratch(),
        compiler_params=pltpu.CompilerParams(
            collective_id=0, has_side_effects=True, vmem_limit_bytes=56 * 2**20
        ),
    )(inputs[0], hidden_one[0], hidden_two[0], outputs[0], cotangent[0], w_in, w_mid, w_out)
    gi, d_in, d_mid, d_out, b_hidden, b_out = pl.pallas_call(
        finish,
        out_shape=[
            jax.ShapeDtypeStruct((BAND, W, C), BF16),
            jax.ShapeDtypeStruct((4, M), F32),
            jax.ShapeDtypeStruct((3, 3, M), F32),
            jax.ShapeDtypeStruct((4, M), F32),
            jax.ShapeDtypeStruct((2,), F32),
            jax.ShapeDtypeStruct((4,), F32),
        ],
        in_specs=[anywhere] * 5,
        out_specs=[anywhere] * 6,
        scratch_shapes=[
            pltpu.VMEM((BAND, W, C), BF16),
            pltpu.VMEM((DEPTH, 128), F32),
            pltpu.VMEM((DEPTH, 128), F32),
            pltpu.VMEM((DEPTH, 128), F32),
            pltpu.VMEM((8, 128), F32),
            pltpu.VMEM((4, M), F32),
            pltpu.VMEM((3, 3, M), F32),
            pltpu.VMEM((4, M), F32),
            pltpu.VMEM((2,), F32),
            pltpu.VMEM((4,), F32),
            pltpu.SemaphoreType.DMA((BAND + 4,)),
            pltpu.SemaphoreType.DMA((BAND + 5,)),
        ],
    )(gi, f0, f1, f2, f3)
    return gi[None], d_in, d_mid, d_out.T, b_hidden, b_out


def solution(mesh):
    placed = (
        P("tm", "rows", None, None),
        P("tm", "rows", None, None),
        P("tm", "rows", None, None),
        P("tm", "rows", None, None),
        P("tm", "rows", None, None),
        P(),
        P(),
        P(),
    )
    return jax.shard_map(
        on_device,
        mesh=mesh,
        in_specs=placed,
        out_specs=(
            P("tm", "rows", None, None),
            P(("tm", "rows"), None),
            P(None, None, ("tm", "rows")),
            P(None, ("tm", "rows")),
            P(("tm", "rows")),
            P(("tm", "rows")),
        ),
        check_vma=False,
    )
```

```python
import jax
import jax.numpy as jnp
from jax import lax
from jax.experimental import pallas as pl
from jax.experimental.pallas import tpu as pltpu
from jax.sharding import PartitionSpec as P

F32 = jnp.float32
BF16 = jnp.bfloat16
MESH = pl.DeviceIdType.MESH

BAND = 4
W = 120
WP = 128
NP = BAND * WP
C = 1024
M = 256
E = C // 8
PIECES = ((4, 3), (3, 3), (5, 0))
DEPTH = 16


def dot_t0(a, b):
    return lax.dot_general(a, b, (((0,), (0,)), ((), ())), preferred_element_type=F32)


def dot_t1(a, b):
    return lax.dot_general(a, b, (((1,), (1,)), ((), ())), preferred_element_type=F32)


def pad_rows(value):
    return jnp.concatenate([value, jnp.zeros((WP - W, value.shape[1]), F32)], 0).astype(BF16)


def kernel(
    inp, h1, h2, outp, cot, w_in, w_mid, w_out,
    gi, f0_out, f1_out, f2_out, f3_out,
    inp_v, h1_v, h2_v, outp_v, cot_v, win_v, wmid_v, wout_v,
    og, og_t, h2o, h1p, h1_t, m3, in_t, edge_t, first, mid_s, edge_mid, mup, mdn,
    prod_e, prod_l, got_e, got_l, back, d0, kf, d2, bo, bh,
    cs0, cr0, a1s0, a1r0, b1s0, b1r0, a2s0, a2r0, b2s0, b2r0, zf0, zs0, zr0,
    cs1, cr1, a1s1, a1r1, b1s1, b1r1, a2s1, a2r1, b2s1, b2r1, zf1, zs1, zr1,
    cs2, cr2, xys2, xyr2, zf2, zs2, zr2, zf3, zs3, zr3, sum3, xys3, xyr3,
    load_sem, send_sem, recv_sem,
):
    tm = lax.axis_index("tm")
    rows = lax.axis_index("rows")
    n_tm = lax.axis_size("tm")
    n_rows = lax.axis_size("rows")
    core = tm % 2
    mx = (tm // 2) % 4
    my = (tm // 8) * 2 + rows % 2
    mz = rows // 2

    def at(x, y, z, c):
        return (((y // 2) * 4 + x) * 2 + c, z * 2 + y % 2)

    sibling = at(mx, my, mz, 1 - core)
    xy_peer = {(i, j): at((mx + i) % 4, (my + j) % 4, mz, core) for i in range(4) for j in range(4) if i + j}
    x_peer = [xy_peer[k, 0] for k in range(1, 4)]
    y_peer = [xy_peer[0, k] for k in range(1, 4)]
    z_peer = [at(mx, my, (mz + k) % 8, core) for k in range(1, 8)]
    tm_next = ((tm + 1) % n_tm, rows)
    tm_prev = ((tm + n_tm - 1) % n_tm, rows)
    row_next = (tm, (rows + 1) % n_rows)
    row_prev = (tm, (rows + n_rows - 1) % n_rows)

    loads = []
    for i, (src, dst) in enumerate(
        ((outp, outp_v), (cot, cot_v), (w_out, wout_v), (h2, h2_v), (h1, h1_v), (inp, inp_v), (w_mid, wmid_v), (w_in, win_v))
    ):
        copy = pltpu.make_async_copy(src, dst, load_sem.at[i])
        copy.start()
        loads.append(copy)

    barrier = pltpu.get_barrier_semaphore()
    partners = [sibling, *xy_peer.values(), *z_peer, tm_next, tm_prev, row_next, row_prev]
    for peer in partners:
        pl.semaphore_signal(barrier, inc=1, device_id=peer, device_id_type=MESH)

    counter = [0]

    def send(src, dst, peer):
        i = counter[0]
        counter[0] += 1
        copy = pltpu.make_async_remote_copy(
            src_ref=src, dst_ref=dst, send_sem=send_sem.at[i], recv_sem=recv_sem.at[i],
            device_id=peer, device_id_type=MESH,
        )
        copy.start()
        return copy

    def dot(a, b):
        return jnp.dot(a, b, preferred_element_type=F32)

    def halves(held, value, *shape):
        for h in range(value.shape[1] // 128):
            held[h] = value[:, h * 128 : (h + 1) * 128].reshape(*shape, 128)

    def as_column(value):
        total = jnp.sum(value.astype(F32), 0, keepdims=True)
        return jnp.broadcast_to(total, (WP, M)).T.reshape(8, 32, WP)

    for copy in loads[:4]:
        copy.wait()
    for r in range(BAND):
        grad = jnp.where(outp_v[r].astype(F32) > 0, cot_v[r].astype(F32), 0.0)
        og[r * WP : (r + 1) * WP, :] = pad_rows(grad)
        h2o[r * WP : (r + 1) * WP, 0:M] = pad_rows(h2_v[r].astype(F32))
    h2o[:, M:] = jnp.ones((NP, WP), BF16)
    mid32 = jnp.where(h2o[:, 0:M].astype(F32) > 0, dot_t1(og[...], wout_v[...]), 0.0)
    mid = mid32.astype(BF16)
    mid_s[...] = mid
    edge_mid[0] = jnp.where(rows < n_rows - 1, mid32[NP - WP :], 0.0).astype(BF16)
    edge_mid[1] = jnp.where(rows > 0, mid32[:WP], 0.0).astype(BF16)
    m3[WP : WP + NP, 0:M] = pltpu.roll(mid32, NP - 1, 0).astype(BF16)
    m3[WP : WP + NP, M : 2 * M] = mid
    m3[WP : WP + NP, 2 * M : 3 * M] = pltpu.roll(mid32, 1, 0).astype(BF16)

    og_t[...] = og[...].T
    grad = dot(og_t[...], h2o[...])
    halves(d0, grad[:, 0:M], 16, 64)
    bo[...] = grad[:, M:].reshape(16, 64, WP)
    bh[8:16] = as_column(mid)
    loads[4].wait()
    for r in range(BAND):
        h1p[r * WP : (r + 1) * WP, :] = pad_rows(h1_v[r].astype(F32))
    h1_t[...] = h1p[...].T
    halves(kf.at[pl.ds(6, 6)], dot(h1_t[...], m3[WP : WP + NP, :]), 16, 16)
    loads[5].wait()
    for r in range(BAND):
        part = slice(r * WP, (r + 1) * WP)
        value = pad_rows(inp_v[r].astype(F32)).T
        edge_t[0, :, part] = jnp.where(tm < n_tm - 1, value[0:E].astype(F32), 0.0).astype(BF16)
        edge_t[1, :, part] = jnp.where(tm > 0, value[E : 2 * E].astype(F32), 0.0).astype(BF16)
        in_t[2 * E :, part] = value[2 * E :]

    pl.semaphore_wait(barrier, len(partners))
    mid_down = send(edge_mid.at[0], mup, row_next)
    mid_up = send(edge_mid.at[1], mdn, row_prev)
    in_next = send(edge_t.at[0], in_t.at[pl.ds(0, E)], tm_next)
    in_prev = send(edge_t.at[1], in_t.at[pl.ds(E, E)], tm_prev)

    def slab(piece, t, low, s):
        if piece == 0 and s >= 4 or piece == 1:
            tap = s - 1 if piece == 0 else s if s < 3 else s + 3
            parts = [kf[2 * tap + h, t, pl.ds(low, 8, stride=2), :] for h in range(2)]
        elif piece == 0 or s != 2:
            held, j = (d0, s) if piece == 0 else (d2, s - s // 3)
            parts = [held[h, t, pl.ds(4 * low + j, 8, stride=8), :] for h in range(2)]
        else:
            lane = lax.broadcasted_iota(jnp.int32, (8, 128), 1)
            total = jnp.zeros((8, 128), F32)
            for j in range(4):
                total = jnp.where(lane == j, bo[t, pl.ds(4 * low + j, 8, stride=8), :], total)
            for j in range(2):
                total = jnp.where(lane == 4 + j, bh[t, pl.ds(2 * low + j, 8, stride=4), :], total)
            parts = [total, jnp.zeros((8, 128), F32)]
        return jnp.concatenate(parts, 0)

    def two_terms(value):
        total = value[0:8] + value[8:16]
        head = total.astype(BF16).astype(F32)
        return jnp.concatenate([head, total - head], 0)

    bufs = (
        (cs0, cr0, a1s0, a1r0, b1s0, b1r0, a2s0, a2r0, b2s0, b2r0, zf0, zs0, zr0),
        (cs1, cr1, a1s1, a1r1, b1s1, b1r1, a2s1, a2r1, b2s1, b2r1, zf1, zs1, zr1),
        (cs2, cr2, xys2, xyr2, None, None, None, None, None, None, zf2, zs2, zr2),
    )

    late3 = []

    def core_phase(p):
        na, nb = PIECES[p]
        cs, cr = bufs[p][:2]

        def body(x, carry):
            for y in range(4):
                t = ((y // 2) * 4 + x) * 2 + (1 - core)
                for s in range(na + nb):
                    value = slab(p, t, y % 2, s)
                    if p == 2 and s == 2:
                        value = two_terms(value)
                    cs[x, y, s] = value.astype(BF16)
            return carry

        lax.fori_loop(0, 4, body, 0)
        return [send(cs, cr, sibling)]

    def first_phase(p, copies):
        na, nb = PIECES[p]
        cs, cr, a1s, a1r, b1s, b1r = bufs[p][:6]
        for copy in copies:
            copy.wait()

        def body(x, carry):
            for y in range(4):
                t = ((y // 2) * 4 + x) * 2 + core
                for s in range(na + nb):
                    value = slab(p, t, y % 2, s) + cr[x, y, s].astype(F32)
                    if p == 2 and s == 2:
                        value = two_terms(value)
                    if p == 2 and s > 2:
                        for h in range(2):
                            row = x * 16 + y * 4 + 2 * (s - 3) + h
                            zf3[pl.ds(row, 8, stride=64), :] = value[8 * h : 8 * h + 8]
                    elif s < na:
                        a1s[x, y, s] = value.astype(BF16)
                    else:
                        b1s[y, x, s - na] = value.astype(BF16)
            return carry

        lax.fori_loop(0, 4, body, 0)
        out = []
        if p == 2:
            zs3[...] = zf3[...].reshape(8, 64, 128).astype(BF16)
            for k in (4, 3, 5, 2, 6, 1, 7):
                late3.append(send(zs3.at[(mz + k) % 8], zr3.at[k - 1], z_peer[k - 1]))
            for (i, j), peer in sorted(xy_peer.items(), key=lambda item: -(item[0][0] % 3 + item[0][1] % 3)):
                out.append(send(a1s.at[(mx + i) % 4, (my + j) % 4], a1r.at[4 * i + j - 1], peer))
            return out
        for k in (2, 1, 3):
            out.append(send(a1s.at[(mx + k) % 4], a1r.at[k - 1], x_peer[k - 1]))
            out.append(send(b1s.at[(my + k) % 4], b1r.at[k - 1], y_peer[k - 1]))
        return out

    def gathered(own, held, got, j):
        total = held[own, j].astype(F32)
        for k in range(3):
            total = total + got[k, j].astype(F32)
        return total

    def second_phase(p, copies):
        na, nb = PIECES[p]
        _, _, a1s, a1r, b1s, b1r, a2s, a2r, b2s, b2r = bufs[p][:10]
        for copy in copies:
            copy.wait()
        for j in range(4):
            a2s[j] = gathered(mx, a1s, a1r, j).astype(BF16)
            b2s[j] = gathered(my, b1s, b1r, j).astype(BF16)
        out = []
        for k in (2, 1, 3):
            out.append(send(a2s.at[(my + k) % 4], a2r.at[k - 1], y_peer[k - 1]))
            out.append(send(b2s.at[(mx + k) % 4], b2r.at[k - 1], x_peer[k - 1]))
        return out

    def third_phase(p, copies):
        na, nb = PIECES[p]
        _, _, xys, xyr, _, _, a2s, a2r, b2s, b2r, zf, zs, zr = bufs[p]
        for copy in copies:
            copy.wait()
        for s in range(3 if p == 2 else na + nb):
            if p == 2:
                total = xys[mx, my, s].astype(F32)
                for k in range(15):
                    total = total + xyr[k, s].astype(F32)
                if s == 2:
                    total = two_terms(total)
            else:
                own, held, got, j = (my, a2s, a2r, s) if s < na else (mx, b2s, b2r, s - na)
                total = gathered(own, held, got, j)
            for h in range(2):
                zf[pl.ds(2 * s + h, 8, stride=DEPTH), :] = total[8 * h : 8 * h + 8]
        zs[...] = zf[...].reshape(8, DEPTH, 128).astype(BF16)
        return [send(zs.at[(mz + k) % 8], zr.at[k - 1], z_peer[k - 1]) for k in (4, 3, 5, 2, 6, 1, 7)]

    def last_phase(p, copies, result):
        zf, _, zr = bufs[p][10:]
        for copy in copies:
            copy.wait()
        total = zf[pl.ds(pl.multiple_of(mz * DEPTH, 8), DEPTH), :]
        for k in range(7):
            total = total + zr[k].astype(F32)
        result[...] = total

    def cross_phase(copies):
        for copy in copies:
            copy.wait()
        total = zs3[mz].astype(F32)
        for k in range(7):
            total = total + zr3[k].astype(F32)
        sum3[0:64, :] = total
        for i in range(16):
            xys3[i] = sum3[4 * i : 4 * i + 8, :]
        out = []
        for (i, j), peer in sorted(xy_peer.items(), key=lambda item: -(item[0][0] % 3 + item[0][1] % 3)):
            out.append(send(xys3.at[((mx + i) % 4) * 4 + (my + j) % 4], xyr3.at[4 * i + j - 1], peer))
        return out

    def cross_end(copies, result):
        for copy in copies:
            copy.wait()
        total = xys3[mx * 4 + my]
        for k in range(15):
            total = total + xyr3[k]
        result[...] = total

    flight0 = core_phase(0)

    def back_of(start, count, a):
        total = None
        for b in range(3):
            term = dot_t1(m3[start : start + count, b * M : (b + 1) * M], wmid_v[a, b])
            total = term if total is None else total + term
        return total

    loads[6].wait()
    back[...] = back_of(WP, NP, 1)
    back[0 : NP - WP, :] += back_of(2 * WP, NP - WP, 0)
    back[WP:NP, :] += back_of(WP, NP - WP, 2)

    flight0 = first_phase(0, flight0)
    halves(kf.at[pl.ds(0, 6)], dot(h1_t[:, 0 : NP - WP], m3[2 * WP : WP + NP, :]), 16, 16)
    halves(kf.at[pl.ds(12, 6)], dot(h1_t[:, WP:NP], m3[WP:NP, :]), 16, 16)

    mid_down.wait()
    mid_up.wait()
    for held, start in ((mup, 0), (mdn, NP + WP)):
        value = held[...].astype(F32)
        m3[start : start + WP, 0:M] = pltpu.roll(value, WP - 1, 0).astype(BF16)
        m3[start : start + WP, M : 2 * M] = held[...]
        m3[start : start + WP, 2 * M : 3 * M] = pltpu.roll(value, 1, 0).astype(BF16)
    for first_tap, grad in (
        (0, dot(h1_t[:, NP - WP :], m3[NP + WP :, :])),
        (12, dot(h1_t[:, 0:WP], m3[0:WP, :])),
    ):
        for h in range(6):
            kf[first_tap + h] += grad[:, h * 128 : (h + 1) * 128].reshape(16, 16, 128)
    flight1 = core_phase(1)

    back[0:WP, :] += back_of(0, WP, 2)
    back[NP - WP : NP, :] += back_of(NP + WP, WP, 0)
    first_grad = jnp.where(h1p[...].astype(F32) > 0, back[...], 0.0).astype(BF16)
    first[...] = first_grad
    flight1 = first_phase(1, flight1)
    bh[0:8] = as_column(first_grad)
    in_next.wait()
    in_prev.wait()
    halves(d2, dot(in_t[...], first[...]), 16, 64)
    flight2 = core_phase(2)

    loads[7].wait()
    edge = dot_t1(first[...], win_v[0 : 2 * E, :])
    prod_e[...] = jnp.where(tm > 0, edge[:, 0:E], 0.0).astype(BF16)
    prod_l[...] = jnp.where(tm < n_tm - 1, edge[:, E:], 0.0).astype(BF16)
    early = send(prod_e, got_e, tm_prev)
    late = send(prod_l, got_l, tm_next)
    flight2 = first_phase(2, flight2)

    rest = og[:, 2 * E :].astype(F32) + dot_t1(first[...], win_v[2 * E :, :])
    for r in range(BAND):
        gi[r, :, 2 * E :] = rest[r * WP : r * WP + W].astype(BF16)
    flight0 = second_phase(0, flight0)
    flight1 = second_phase(1, flight1)
    flight0 = third_phase(0, flight0)
    early.wait()
    late.wait()
    for r in range(BAND):
        part = slice(r * WP, r * WP + WP)
        one = og[part, 0:E].astype(F32) + got_e[part, :].astype(F32)
        two = og[part, E : 2 * E].astype(F32) + got_l[part, :].astype(F32)
        gi[r, :, 0:E] = one[:W].astype(BF16)
        gi[r, :, E : 2 * E] = two[:W].astype(BF16)


    flight2 = third_phase(2, flight2)
    flight3 = cross_phase(late3)
    flight1 = third_phase(1, flight1)
    last_phase(0, flight0, f0_out)
    last_phase(2, flight2, f2_out)
    cross_end(flight3, f3_out)
    last_phase(1, flight1, f1_out)


def scratch():
    def v(*shape, dtype=BF16):
        return pltpu.VMEM(shape, dtype)

    shapes = [
        v(BAND, W, C), v(BAND, W, M), v(BAND, W, M), v(BAND, W, C), v(BAND, W, C),
        v(C, M), v(3, 3, M, M), v(M, C),
        v(NP, C), v(C, NP), v(NP, M + WP), v(NP, M), v(M, NP), v(NP + 2 * WP, 3 * M),
        v(C, NP), v(2, E, NP), v(NP, M), v(NP, M), v(2, WP, M), v(WP, M), v(WP, M),
        v(NP, E), v(NP, E), v(NP, E), v(NP, E),
        v(NP, M, dtype=F32), v(2, 16, 64, 128, dtype=F32), v(18, 16, 16, 128, dtype=F32), v(2, 16, 64, 128, dtype=F32),
        v(16, 64, WP, dtype=F32), v(16, 32, WP, dtype=F32),
    ]
    tile = (16, 128)
    for na, nb in PIECES:
        shapes += [v(4, 4, na + nb, *tile), v(4, 4, na + nb, *tile)]
        if nb:
            shapes += [v(4, 4, na, *tile), v(3, 4, na, *tile), v(4, 4, nb, *tile), v(3, 4, nb, *tile)]
            shapes += [v(4, na, *tile), v(3, na, *tile), v(4, nb, *tile), v(3, nb, *tile)]
        else:
            shapes += [v(4, 4, 3, *tile), v(15, 3, *tile)]
        shapes += [v(8 * DEPTH, 128, dtype=F32), v(8, DEPTH, 128), v(7, DEPTH, 128)]
    shapes += [v(8 * 64, 128, dtype=F32), v(8, 64, 128), v(7, 64, 128)]
    shapes += [v(72, 128, dtype=F32), v(16, 8, 128, dtype=F32), v(15, 8, 128, dtype=F32)]
    shapes += [pltpu.SemaphoreType.DMA((9,)), pltpu.SemaphoreType.DMA((100,)), pltpu.SemaphoreType.DMA((100,))]
    return shapes


def finish(
    held, f0, f1, f2, f3, gi, d_in, d_mid, d_out, b_hidden, b_out,
    d_in_v, d_mid_v, d_out_v, b_hidden_v, b_out_v, store_sem,
):
    results = [(d_in_v, d_in), (d_mid_v, d_mid), (d_out_v, d_out), (b_hidden_v, b_hidden), (b_out_v, b_out)]
    results = [(held.at[r], gi.at[r]) for r in range(BAND)] + results
    stores = [pltpu.make_async_copy(src, dst, store_sem.at[i]) for i, (src, dst) in enumerate(results)]

    def lines(ref, start, count):
        return jnp.concatenate([ref[pl.ds(2 * start + h, count, stride=2), :] for h in range(2)], 1)

    for store in stores[:BAND]:
        store.start()
    d_in_v[0:2, :] = lines(f2, 0, 2)
    d_in_v[2:4, :] = lines(f3, 0, 2)
    d_mid_v[0] = lines(f1, 0, 3)
    d_mid_v[1] = lines(f0, 4, 3)
    d_mid_v[2] = lines(f1, 3, 3)
    d_out_v[...] = lines(f0, 0, 4)
    bias = f2[4, :] + f2[5, :]
    b_hidden_v[...] = bias[4:6]
    b_out_v[...] = bias[0:4]
    for store in stores[BAND:]:
        store.start()
    for store in stores:
        store.wait()


def on_device(inputs, hidden_one, hidden_two, outputs, cotangent, w_in, w_mid, w_out):
    anywhere = pl.BlockSpec(memory_space=pl.ANY)
    vmem = pl.BlockSpec(memory_space=pltpu.VMEM)
    gi, f0, f1, f2, f3 = pl.pallas_call(
        kernel,
        out_shape=[
            pltpu.VMEM((BAND, W, C), BF16),
            pltpu.VMEM((DEPTH, 128), F32),
            pltpu.VMEM((DEPTH, 128), F32),
            pltpu.VMEM((DEPTH, 128), F32),
            pltpu.VMEM((8, 128), F32),
        ],
        in_specs=[anywhere] * 8,
        out_specs=[vmem] * 5,
        scratch_shapes=scratch(),
        compiler_params=pltpu.CompilerParams(
            collective_id=0, has_side_effects=True, vmem_limit_bytes=56 * 2**20
        ),
    )(inputs[0], hidden_one[0], hidden_two[0], outputs[0], cotangent[0], w_in, w_mid, w_out)
    gi, d_in, d_mid, d_out, b_hidden, b_out = pl.pallas_call(
        finish,
        out_shape=[
            jax.ShapeDtypeStruct((BAND, W, C), BF16),
            jax.ShapeDtypeStruct((4, M), F32),
            jax.ShapeDtypeStruct((3, 3, M), F32),
            jax.ShapeDtypeStruct((4, M), F32),
            jax.ShapeDtypeStruct((2,), F32),
            jax.ShapeDtypeStruct((4,), F32),
        ],
        in_specs=[vmem] * 5,
        out_specs=[anywhere] * 6,
        scratch_shapes=[
            pltpu.VMEM((4, M), F32),
            pltpu.VMEM((3, 3, M), F32),
            pltpu.VMEM((4, M), F32),
            pltpu.VMEM((2,), F32),
            pltpu.VMEM((4,), F32),
            pltpu.SemaphoreType.DMA((BAND + 5,)),
        ],
        compiler_params=pltpu.CompilerParams(vmem_limit_bytes=8 * 2**20),
    )(gi, f0, f1, f2, f3)
    return gi[None], d_in, d_mid, d_out.T, b_hidden, b_out


def solution(mesh):
    placed = (
        P("tm", "rows", None, None),
        P("tm", "rows", None, None),
        P("tm", "rows", None, None),
        P("tm", "rows", None, None),
        P("tm", "rows", None, None),
        P(),
        P(),
        P(),
    )
    return jax.shard_map(
        on_device,
        mesh=mesh,
        in_specs=placed,
        out_specs=(
            P("tm", "rows", None, None),
            P(("tm", "rows"), None),
            P(None, None, ("tm", "rows")),
            P(None, ("tm", "rows")),
            P(("tm", "rows")),
            P(("tm", "rows")),
        ),
        check_vma=False,
    )
```

```python
import jax
import jax.numpy as jnp
from jax import lax
from jax.experimental import pallas as pl
from jax.experimental.pallas import tpu as pltpu
from jax.sharding import PartitionSpec as P

F32 = jnp.float32
BF16 = jnp.bfloat16
MESH = pl.DeviceIdType.MESH

BAND = 4
W = 120
WP = 128
NP = BAND * WP
C = 1024
M = 256
E = C // 8
PIECES = ((4, 3), (3, 3), (5, 0))
DEPTH = 16


def dot_t0(a, b):
    return lax.dot_general(a, b, (((0,), (0,)), ((), ())), preferred_element_type=F32)


def dot_t1(a, b):
    return lax.dot_general(a, b, (((1,), (1,)), ((), ())), preferred_element_type=F32)


def pad_rows(value):
    return jnp.concatenate([value, jnp.zeros((WP - W, value.shape[1]), F32)], 0).astype(BF16)


def kernel(
    inp, h1, h2, outp, cot, w_in, w_mid, w_out,
    gi, f0_out, f1_out, f2_out, f3_out,
    inp_v, h1_v, h2_v, outp_v, cot_v, win_v, wmid_v, wout_v,
    og, og_t, h2o, h1p, h1_t, m3, in_t, edge_t, first, mid_s, edge_mid, mup, mdn,
    prod_e, prod_l, got_e, got_l, back, d0, kf, d2, bo, bh,
    cs0, cr0, a1s0, a1r0, b1s0, b1r0, a2s0, a2r0, b2s0, b2r0, zf0, zs0, zr0,
    cs1, cr1, a1s1, a1r1, b1s1, b1r1, a2s1, a2r1, b2s1, b2r1, zf1, zs1, zr1,
    cs2, cr2, xys2, xyr2, zf2, zs2, zr2, zf3, zs3, zr3, sum3, xys3, xyr3,
    load_sem, send_sem, recv_sem,
):
    tm = lax.axis_index("tm")
    rows = lax.axis_index("rows")
    n_tm = lax.axis_size("tm")
    n_rows = lax.axis_size("rows")
    core = tm % 2
    mx = (tm // 2) % 4
    my = (tm // 8) * 2 + rows % 2
    mz = rows // 2

    def at(x, y, z, c):
        return (((y // 2) * 4 + x) * 2 + c, z * 2 + y % 2)

    sibling = at(mx, my, mz, 1 - core)
    xy_peer = {(i, j): at((mx + i) % 4, (my + j) % 4, mz, core) for i in range(4) for j in range(4) if i + j}
    x_peer = [xy_peer[k, 0] for k in range(1, 4)]
    y_peer = [xy_peer[0, k] for k in range(1, 4)]
    z_peer = [at(mx, my, (mz + k) % 8, core) for k in range(1, 8)]
    tm_next = ((tm + 1) % n_tm, rows)
    tm_prev = ((tm + n_tm - 1) % n_tm, rows)
    row_next = (tm, (rows + 1) % n_rows)
    row_prev = (tm, (rows + n_rows - 1) % n_rows)

    loads = []
    for i, (src, dst) in enumerate(
        ((outp, outp_v), (cot, cot_v), (w_out, wout_v), (h2, h2_v), (h1, h1_v), (inp, inp_v), (w_mid, wmid_v), (w_in, win_v))
    ):
        copy = pltpu.make_async_copy(src, dst, load_sem.at[i])
        copy.start()
        loads.append(copy)

    barrier = pltpu.get_barrier_semaphore()
    partners = [sibling, *xy_peer.values(), *z_peer, tm_next, tm_prev, row_next, row_prev]
    for peer in partners:
        pl.semaphore_signal(barrier, inc=1, device_id=peer, device_id_type=MESH)

    counter = [0]

    def send(src, dst, peer):
        i = counter[0]
        counter[0] += 1
        copy = pltpu.make_async_remote_copy(
            src_ref=src, dst_ref=dst, send_sem=send_sem.at[i], recv_sem=recv_sem.at[i],
            device_id=peer, device_id_type=MESH,
        )
        copy.start()
        return copy

    def dot(a, b):
        return jnp.dot(a, b, preferred_element_type=F32)

    def halves(held, value, *shape):
        for h in range(value.shape[1] // 128):
            held[h] = value[:, h * 128 : (h + 1) * 128].reshape(*shape, 128)

    def as_column(value):
        total = jnp.sum(value.astype(F32), 0, keepdims=True)
        return jnp.broadcast_to(total, (WP, M)).T.reshape(8, 32, WP)

    for copy in loads[:4]:
        copy.wait()
    for r in range(BAND):
        grad = jnp.where(outp_v[r].astype(F32) > 0, cot_v[r].astype(F32), 0.0)
        og[r * WP : (r + 1) * WP, :] = pad_rows(grad)
        h2o[r * WP : (r + 1) * WP, 0:M] = pad_rows(h2_v[r].astype(F32))
    h2o[:, M:] = jnp.ones((NP, WP), BF16)
    mid32 = jnp.where(h2o[:, 0:M].astype(F32) > 0, dot_t1(og[...], wout_v[...]), 0.0)
    mid = mid32.astype(BF16)
    mid_s[...] = mid
    edge_mid[0] = jnp.where(rows < n_rows - 1, mid32[NP - WP :], 0.0).astype(BF16)
    edge_mid[1] = jnp.where(rows > 0, mid32[:WP], 0.0).astype(BF16)
    m3[WP : WP + NP, 0:M] = pltpu.roll(mid32, NP - 1, 0).astype(BF16)
    m3[WP : WP + NP, M : 2 * M] = mid
    m3[WP : WP + NP, 2 * M : 3 * M] = pltpu.roll(mid32, 1, 0).astype(BF16)

    pl.semaphore_wait(barrier, len(partners))
    mid_down = send(edge_mid.at[0], mup, row_next)
    mid_up = send(edge_mid.at[1], mdn, row_prev)

    loads[5].wait()
    for r in range(BAND):
        part = slice(r * WP, (r + 1) * WP)
        value = pad_rows(inp_v[r].astype(F32)).T
        edge_t[0, :, part] = jnp.where(tm < n_tm - 1, value[0:E].astype(F32), 0.0).astype(BF16)
        edge_t[1, :, part] = jnp.where(tm > 0, value[E : 2 * E].astype(F32), 0.0).astype(BF16)
        in_t[2 * E :, part] = value[2 * E :]
    in_next = send(edge_t.at[0], in_t.at[pl.ds(0, E)], tm_next)
    in_prev = send(edge_t.at[1], in_t.at[pl.ds(E, E)], tm_prev)
    og_t[...] = og[...].T
    grad = dot(og_t[...], h2o[...])
    halves(d0, grad[:, 0:M], 16, 64)
    bo[...] = grad[:, M:].reshape(16, 64, WP)
    bh[8:16] = as_column(mid)
    loads[4].wait()
    for r in range(BAND):
        h1p[r * WP : (r + 1) * WP, :] = pad_rows(h1_v[r].astype(F32))
    h1_t[...] = h1p[...].T
    halves(kf.at[pl.ds(6, 6)], dot(h1_t[...], m3[WP : WP + NP, :]), 16, 16)
    def slab(piece, t, low, s):
        if piece == 0 and s >= 4 or piece == 1:
            tap = s - 1 if piece == 0 else s if s < 3 else s + 3
            parts = [kf[2 * tap + h, t, pl.ds(low, 8, stride=2), :] for h in range(2)]
        elif piece == 0 or s != 2:
            held, j = (d0, s) if piece == 0 else (d2, s - s // 3)
            parts = [held[h, t, pl.ds(4 * low + j, 8, stride=8), :] for h in range(2)]
        else:
            lane = lax.broadcasted_iota(jnp.int32, (8, 128), 1)
            total = jnp.zeros((8, 128), F32)
            for j in range(4):
                total = jnp.where(lane == j, bo[t, pl.ds(4 * low + j, 8, stride=8), :], total)
            for j in range(2):
                total = jnp.where(lane == 4 + j, bh[t, pl.ds(2 * low + j, 8, stride=4), :], total)
            parts = [total, jnp.zeros((8, 128), F32)]
        return jnp.concatenate(parts, 0)

    def two_terms(value):
        total = value[0:8] + value[8:16]
        head = total.astype(BF16).astype(F32)
        return jnp.concatenate([head, total - head], 0)

    bufs = (
        (cs0, cr0, a1s0, a1r0, b1s0, b1r0, a2s0, a2r0, b2s0, b2r0, zf0, zs0, zr0),
        (cs1, cr1, a1s1, a1r1, b1s1, b1r1, a2s1, a2r1, b2s1, b2r1, zf1, zs1, zr1),
        (cs2, cr2, xys2, xyr2, None, None, None, None, None, None, zf2, zs2, zr2),
    )

    late3 = []

    def core_phase(p):
        na, nb = PIECES[p]
        cs, cr = bufs[p][:2]

        def body(x, carry):
            for y in range(4):
                t = ((y // 2) * 4 + x) * 2 + (1 - core)
                for s in range(na + nb):
                    value = slab(p, t, y % 2, s)
                    if p == 2 and s == 2:
                        value = two_terms(value)
                    cs[x, y, s] = value.astype(BF16)
            return carry

        lax.fori_loop(0, 4, body, 0)
        return [send(cs, cr, sibling)]

    def first_phase(p, copies):
        na, nb = PIECES[p]
        cs, cr, a1s, a1r, b1s, b1r = bufs[p][:6]
        for copy in copies:
            copy.wait()

        def body(x, carry):
            for y in range(4):
                t = ((y // 2) * 4 + x) * 2 + core
                for s in range(na + nb):
                    value = slab(p, t, y % 2, s) + cr[x, y, s].astype(F32)
                    if p == 2 and s == 2:
                        value = two_terms(value)
                    if p == 2 and s > 2:
                        for h in range(2):
                            row = x * 16 + y * 4 + 2 * (s - 3) + h
                            zf3[pl.ds(row, 8, stride=64), :] = value[8 * h : 8 * h + 8]
                    elif s < na:
                        a1s[x, y, s] = value.astype(BF16)
                    else:
                        b1s[y, x, s - na] = value.astype(BF16)
            return carry

        lax.fori_loop(0, 4, body, 0)
        out = []
        if p == 2:
            zs3[...] = zf3[...].reshape(8, 64, 128).astype(BF16)
            for k in (4, 3, 5, 2, 6, 1, 7):
                late3.append(send(zs3.at[(mz + k) % 8], zr3.at[k - 1], z_peer[k - 1]))
            for (i, j), peer in sorted(xy_peer.items(), key=lambda item: -(item[0][0] % 3 + item[0][1] % 3)):
                out.append(send(a1s.at[(mx + i) % 4, (my + j) % 4], a1r.at[4 * i + j - 1], peer))
            return out
        for k in (2, 1, 3):
            out.append(send(a1s.at[(mx + k) % 4], a1r.at[k - 1], x_peer[k - 1]))
            out.append(send(b1s.at[(my + k) % 4], b1r.at[k - 1], y_peer[k - 1]))
        return out

    def gathered(own, held, got, j):
        total = held[own, j].astype(F32)
        for k in range(3):
            total = total + got[k, j].astype(F32)
        return total

    def second_phase(p, copies):
        na, nb = PIECES[p]
        _, _, a1s, a1r, b1s, b1r, a2s, a2r, b2s, b2r = bufs[p][:10]
        for copy in copies:
            copy.wait()
        for j in range(4):
            a2s[j] = gathered(mx, a1s, a1r, j).astype(BF16)
            b2s[j] = gathered(my, b1s, b1r, j).astype(BF16)
        out = []
        for k in (2, 1, 3):
            out.append(send(a2s.at[(my + k) % 4], a2r.at[k - 1], y_peer[k - 1]))
            out.append(send(b2s.at[(mx + k) % 4], b2r.at[k - 1], x_peer[k - 1]))
        return out

    def third_phase(p, copies):
        na, nb = PIECES[p]
        _, _, xys, xyr, _, _, a2s, a2r, b2s, b2r, zf, zs, zr = bufs[p]
        for copy in copies:
            copy.wait()
        for s in range(3 if p == 2 else na + nb):
            if p == 2:
                total = xys[mx, my, s].astype(F32)
                for k in range(15):
                    total = total + xyr[k, s].astype(F32)
                if s == 2:
                    total = two_terms(total)
            else:
                own, held, got, j = (my, a2s, a2r, s) if s < na else (mx, b2s, b2r, s - na)
                total = gathered(own, held, got, j)
            for h in range(2):
                zf[pl.ds(2 * s + h, 8, stride=DEPTH), :] = total[8 * h : 8 * h + 8]
        zs[...] = zf[...].reshape(8, DEPTH, 128).astype(BF16)
        return [send(zs.at[(mz + k) % 8], zr.at[k - 1], z_peer[k - 1]) for k in (4, 3, 5, 2, 6, 1, 7)]

    def last_phase(p, copies, result):
        zf, _, zr = bufs[p][10:]
        for copy in copies:
            copy.wait()
        total = zf[pl.ds(pl.multiple_of(mz * DEPTH, 8), DEPTH), :]
        for k in range(7):
            total = total + zr[k].astype(F32)
        result[...] = total

    def cross_phase(copies):
        for copy in copies:
            copy.wait()
        total = zs3[mz].astype(F32)
        for k in range(7):
            total = total + zr3[k].astype(F32)
        sum3[0:64, :] = total
        for i in range(16):
            xys3[i] = sum3[4 * i : 4 * i + 8, :]
        out = []
        for (i, j), peer in sorted(xy_peer.items(), key=lambda item: -(item[0][0] % 3 + item[0][1] % 3)):
            out.append(send(xys3.at[((mx + i) % 4) * 4 + (my + j) % 4], xyr3.at[4 * i + j - 1], peer))
        return out

    def cross_end(copies, result):
        for copy in copies:
            copy.wait()
        total = xys3[mx * 4 + my]
        for k in range(15):
            total = total + xyr3[k]
        result[...] = total

    flight0 = core_phase(0)

    def back_of(start, count, a):
        total = None
        for b in range(3):
            term = dot_t1(m3[start : start + count, b * M : (b + 1) * M], wmid_v[a, b])
            total = term if total is None else total + term
        return total

    loads[6].wait()
    back[...] = back_of(WP, NP, 1)
    back[0 : NP - WP, :] += back_of(2 * WP, NP - WP, 0)
    back[WP:NP, :] += back_of(WP, NP - WP, 2)

    flight0 = first_phase(0, flight0)
    halves(kf.at[pl.ds(0, 6)], dot(h1_t[:, 0 : NP - WP], m3[2 * WP : WP + NP, :]), 16, 16)
    halves(kf.at[pl.ds(12, 6)], dot(h1_t[:, WP:NP], m3[WP:NP, :]), 16, 16)

    mid_down.wait()
    mid_up.wait()
    for held, start in ((mup, 0), (mdn, NP + WP)):
        value = held[...].astype(F32)
        m3[start : start + WP, 0:M] = pltpu.roll(value, WP - 1, 0).astype(BF16)
        m3[start : start + WP, M : 2 * M] = held[...]
        m3[start : start + WP, 2 * M : 3 * M] = pltpu.roll(value, 1, 0).astype(BF16)
    for first_tap, grad in (
        (0, dot(h1_t[:, NP - WP :], m3[NP + WP :, :])),
        (12, dot(h1_t[:, 0:WP], m3[0:WP, :])),
    ):
        for h in range(6):
            kf[first_tap + h] += grad[:, h * 128 : (h + 1) * 128].reshape(16, 16, 128)
    flight1 = core_phase(1)

    back[0:WP, :] += back_of(0, WP, 2)
    back[NP - WP : NP, :] += back_of(NP + WP, WP, 0)
    first_grad = jnp.where(h1p[...].astype(F32) > 0, back[...], 0.0).astype(BF16)
    first[...] = first_grad
    flight1 = first_phase(1, flight1)
    bh[0:8] = as_column(first_grad)
    in_next.wait()
    in_prev.wait()
    halves(d2, dot(in_t[...], first[...]), 16, 64)
    flight2 = core_phase(2)

    loads[7].wait()
    edge = dot_t1(first[...], win_v[0 : 2 * E, :])
    prod_e[...] = jnp.where(tm > 0, edge[:, 0:E], 0.0).astype(BF16)
    prod_l[...] = jnp.where(tm < n_tm - 1, edge[:, E:], 0.0).astype(BF16)
    early = send(prod_e, got_e, tm_prev)
    late = send(prod_l, got_l, tm_next)
    flight2 = first_phase(2, flight2)

    rest = og[:, 2 * E :].astype(F32) + dot_t1(first[...], win_v[2 * E :, :])
    for r in range(BAND):
        gi[r, :, 2 * E :] = rest[r * WP : r * WP + W].astype(BF16)
    flight0 = second_phase(0, flight0)
    flight1 = second_phase(1, flight1)
    flight0 = third_phase(0, flight0)
    early.wait()
    late.wait()
    for r in range(BAND):
        part = slice(r * WP, r * WP + WP)
        one = og[part, 0:E].astype(F32) + got_e[part, :].astype(F32)
        two = og[part, E : 2 * E].astype(F32) + got_l[part, :].astype(F32)
        gi[r, :, 0:E] = one[:W].astype(BF16)
        gi[r, :, E : 2 * E] = two[:W].astype(BF16)


    flight2 = third_phase(2, flight2)
    flight3 = cross_phase(late3)
    flight1 = third_phase(1, flight1)
    last_phase(0, flight0, f0_out)
    last_phase(2, flight2, f2_out)
    cross_end(flight3, f3_out)
    last_phase(1, flight1, f1_out)


def scratch():
    def v(*shape, dtype=BF16):
        return pltpu.VMEM(shape, dtype)

    shapes = [
        v(BAND, W, C), v(BAND, W, M), v(BAND, W, M), v(BAND, W, C), v(BAND, W, C),
        v(C, M), v(3, 3, M, M), v(M, C),
        v(NP, C), v(C, NP), v(NP, M + WP), v(NP, M), v(M, NP), v(NP + 2 * WP, 3 * M),
        v(C, NP), v(2, E, NP), v(NP, M), v(NP, M), v(2, WP, M), v(WP, M), v(WP, M),
        v(NP, E), v(NP, E), v(NP, E), v(NP, E),
        v(NP, M, dtype=F32), v(2, 16, 64, 128, dtype=F32), v(18, 16, 16, 128, dtype=F32), v(2, 16, 64, 128, dtype=F32),
        v(16, 64, WP, dtype=F32), v(16, 32, WP, dtype=F32),
    ]
    tile = (16, 128)
    for na, nb in PIECES:
        shapes += [v(4, 4, na + nb, *tile), v(4, 4, na + nb, *tile)]
        if nb:
            shapes += [v(4, 4, na, *tile), v(3, 4, na, *tile), v(4, 4, nb, *tile), v(3, 4, nb, *tile)]
            shapes += [v(4, na, *tile), v(3, na, *tile), v(4, nb, *tile), v(3, nb, *tile)]
        else:
            shapes += [v(4, 4, 3, *tile), v(15, 3, *tile)]
        shapes += [v(8 * DEPTH, 128, dtype=F32), v(8, DEPTH, 128), v(7, DEPTH, 128)]
    shapes += [v(8 * 64, 128, dtype=F32), v(8, 64, 128), v(7, 64, 128)]
    shapes += [v(72, 128, dtype=F32), v(16, 8, 128, dtype=F32), v(15, 8, 128, dtype=F32)]
    shapes += [pltpu.SemaphoreType.DMA((9,)), pltpu.SemaphoreType.DMA((100,)), pltpu.SemaphoreType.DMA((100,))]
    return shapes


def finish(
    held, f0, f1, f2, f3, gi, d_in, d_mid, d_out, b_hidden, b_out,
    d_in_v, d_mid_v, d_out_v, b_hidden_v, b_out_v, store_sem,
):
    results = [(d_in_v, d_in), (d_mid_v, d_mid), (d_out_v, d_out), (b_hidden_v, b_hidden), (b_out_v, b_out)]
    results = [(held.at[r], gi.at[r]) for r in range(BAND)] + results
    stores = [pltpu.make_async_copy(src, dst, store_sem.at[i]) for i, (src, dst) in enumerate(results)]

    def lines(ref, start, count):
        return jnp.concatenate([ref[pl.ds(2 * start + h, count, stride=2), :] for h in range(2)], 1)

    for store in stores[:BAND]:
        store.start()
    d_in_v[0:2, :] = lines(f2, 0, 2)
    d_in_v[2:4, :] = lines(f3, 0, 2)
    d_mid_v[0] = lines(f1, 0, 3)
    d_mid_v[1] = lines(f0, 4, 3)
    d_mid_v[2] = lines(f1, 3, 3)
    d_out_v[...] = lines(f0, 0, 4)
    bias = f2[4, :] + f2[5, :]
    b_hidden_v[...] = bias[4:6]
    b_out_v[...] = bias[0:4]
    for store in stores[BAND:]:
        store.start()
    for store in stores:
        store.wait()


def on_device(inputs, hidden_one, hidden_two, outputs, cotangent, w_in, w_mid, w_out):
    anywhere = pl.BlockSpec(memory_space=pl.ANY)
    vmem = pl.BlockSpec(memory_space=pltpu.VMEM)
    gi, f0, f1, f2, f3 = pl.pallas_call(
        kernel,
        out_shape=[
            pltpu.VMEM((BAND, W, C), BF16),
            pltpu.VMEM((DEPTH, 128), F32),
            pltpu.VMEM((DEPTH, 128), F32),
            pltpu.VMEM((DEPTH, 128), F32),
            pltpu.VMEM((8, 128), F32),
        ],
        in_specs=[anywhere] * 8,
        out_specs=[vmem] * 5,
        scratch_shapes=scratch(),
        compiler_params=pltpu.CompilerParams(
            collective_id=0, has_side_effects=True, vmem_limit_bytes=56 * 2**20
        ),
    )(inputs[0], hidden_one[0], hidden_two[0], outputs[0], cotangent[0], w_in, w_mid, w_out)
    gi, d_in, d_mid, d_out, b_hidden, b_out = pl.pallas_call(
        finish,
        out_shape=[
            jax.ShapeDtypeStruct((BAND, W, C), BF16),
            jax.ShapeDtypeStruct((4, M), F32),
            jax.ShapeDtypeStruct((3, 3, M), F32),
            jax.ShapeDtypeStruct((4, M), F32),
            jax.ShapeDtypeStruct((2,), F32),
            jax.ShapeDtypeStruct((4,), F32),
        ],
        in_specs=[vmem] * 5,
        out_specs=[anywhere] * 6,
        scratch_shapes=[
            pltpu.VMEM((4, M), F32),
            pltpu.VMEM((3, 3, M), F32),
            pltpu.VMEM((4, M), F32),
            pltpu.VMEM((2,), F32),
            pltpu.VMEM((4,), F32),
            pltpu.SemaphoreType.DMA((BAND + 5,)),
        ],
        compiler_params=pltpu.CompilerParams(vmem_limit_bytes=8 * 2**20),
    )(gi, f0, f1, f2, f3)
    return gi[None], d_in, d_mid, d_out.T, b_hidden, b_out


def solution(mesh):
    placed = (
        P("tm", "rows", None, None),
        P("tm", "rows", None, None),
        P("tm", "rows", None, None),
        P("tm", "rows", None, None),
        P("tm", "rows", None, None),
        P(),
        P(),
        P(),
    )
    return jax.shard_map(
        on_device,
        mesh=mesh,
        in_specs=placed,
        out_specs=(
            P("tm", "rows", None, None),
            P(("tm", "rows"), None),
            P(None, None, ("tm", "rows")),
            P(None, ("tm", "rows")),
            P(("tm", "rows")),
            P(("tm", "rows")),
        ),
        check_vma=False,
    )
```

```python
import jax
import jax.numpy as jnp
from jax import lax
from jax.experimental import pallas as pl
from jax.experimental.pallas import tpu as pltpu
from jax.sharding import PartitionSpec as P

F32 = jnp.float32
BF16 = jnp.bfloat16
MESH = pl.DeviceIdType.MESH

BAND = 4
W = 120
WP = 128
NP = BAND * WP
C = 1024
M = 256
E = C // 8
PIECES = ((4, 3), (3, 3), (5, 0))
DEPTH = 16


def dot_t0(a, b):
    return lax.dot_general(a, b, (((0,), (0,)), ((), ())), preferred_element_type=F32)


def dot_t1(a, b):
    return lax.dot_general(a, b, (((1,), (1,)), ((), ())), preferred_element_type=F32)


def pad_rows(value):
    return jnp.concatenate([value, jnp.zeros((WP - W, value.shape[1]), F32)], 0).astype(BF16)


def kernel(
    inp, h1, h2, outp, cot, w_in, w_mid, w_out,
    gi, f0_out, f1_out, f2_out, f3_out,
    inp_v, h1_v, h2_v, outp_v, cot_v, win_v, wmid_v, wout_v,
    og, og_t, h2o, h1p, h1_t, m3, in_t, edge_t, first, mid_s, edge_mid, mup, mdn,
    prod_e, prod_l, got_e, got_l, back, d0, kf, d2, bo, bh,
    cs0, cr0, a1s0, a1r0, b1s0, b1r0, a2s0, a2r0, b2s0, b2r0, zf0, zs0, zr0,
    cs1, cr1, a1s1, a1r1, b1s1, b1r1, a2s1, a2r1, b2s1, b2r1, zf1, zs1, zr1,
    cs2, cr2, xys2, xyr2, zf2, zs2, zr2, zf3, zs3, zr3, sum3, xys3, xyr3,
    load_sem, send_sem, recv_sem,
):
    tm = lax.axis_index("tm")
    rows = lax.axis_index("rows")
    n_tm = lax.axis_size("tm")
    n_rows = lax.axis_size("rows")
    core = tm % 2
    mx = (tm // 2) % 4
    my = (tm // 8) * 2 + rows % 2
    mz = rows // 2

    def at(x, y, z, c):
        return (((y // 2) * 4 + x) * 2 + c, z * 2 + y % 2)

    sibling = at(mx, my, mz, 1 - core)
    xy_peer = {(i, j): at((mx + i) % 4, (my + j) % 4, mz, core) for i in range(4) for j in range(4) if i + j}
    x_peer = [xy_peer[k, 0] for k in range(1, 4)]
    y_peer = [xy_peer[0, k] for k in range(1, 4)]
    z_peer = [at(mx, my, (mz + k) % 8, core) for k in range(1, 8)]
    tm_next = ((tm + 1) % n_tm, rows)
    tm_prev = ((tm + n_tm - 1) % n_tm, rows)
    row_next = (tm, (rows + 1) % n_rows)
    row_prev = (tm, (rows + n_rows - 1) % n_rows)

    loads = []
    for i, (src, dst) in enumerate(
        ((outp, outp_v), (cot, cot_v), (w_out, wout_v), (h2, h2_v), (h1, h1_v), (inp, inp_v), (w_mid, wmid_v), (w_in, win_v))
    ):
        copy = pltpu.make_async_copy(src, dst, load_sem.at[i])
        copy.start()
        loads.append(copy)

    barrier = pltpu.get_barrier_semaphore()
    partners = [sibling, *xy_peer.values(), *z_peer, tm_next, tm_prev, row_next, row_prev]
    for peer in partners:
        pl.semaphore_signal(barrier, inc=1, device_id=peer, device_id_type=MESH)

    counter = [0]

    def send(src, dst, peer):
        i = counter[0]
        counter[0] += 1
        copy = pltpu.make_async_remote_copy(
            src_ref=src, dst_ref=dst, send_sem=send_sem.at[i], recv_sem=recv_sem.at[i],
            device_id=peer, device_id_type=MESH,
        )
        copy.start()
        return copy

    def dot(a, b):
        return jnp.dot(a, b, preferred_element_type=F32)

    def halves(held, value, *shape):
        for h in range(value.shape[1] // 128):
            held[h] = value[:, h * 128 : (h + 1) * 128].reshape(*shape, 128)

    def as_column(value):
        total = jnp.sum(value.astype(F32), 0, keepdims=True)
        return jnp.broadcast_to(total, (WP, M)).T.reshape(8, 32, WP)

    for copy in loads[:4]:
        copy.wait()
    for r in range(BAND):
        grad = jnp.where(outp_v[r].astype(F32) > 0, cot_v[r].astype(F32), 0.0)
        og[r * WP : (r + 1) * WP, :] = pad_rows(grad)
        h2o[r * WP : (r + 1) * WP, 0:M] = pad_rows(h2_v[r].astype(F32))
    h2o[:, M:] = jnp.ones((NP, WP), BF16)
    mid32 = jnp.where(h2o[:, 0:M].astype(F32) > 0, dot_t1(og[...], wout_v[...]), 0.0)
    mid = mid32.astype(BF16)
    mid_s[...] = mid
    edge_mid[0] = jnp.where(rows < n_rows - 1, mid32[NP - WP :], 0.0).astype(BF16)
    edge_mid[1] = jnp.where(rows > 0, mid32[:WP], 0.0).astype(BF16)
    m3[WP : WP + NP, 0:M] = pltpu.roll(mid32, NP - 1, 0).astype(BF16)
    m3[WP : WP + NP, M : 2 * M] = mid
    m3[WP : WP + NP, 2 * M : 3 * M] = pltpu.roll(mid32, 1, 0).astype(BF16)

    pl.semaphore_wait(barrier, len(partners))
    mid_down = send(edge_mid.at[0], mup, row_next)
    mid_up = send(edge_mid.at[1], mdn, row_prev)

    loads[5].wait()
    for r in range(BAND):
        part = slice(r * WP, (r + 1) * WP)
        value = pad_rows(inp_v[r].astype(F32)).T
        edge_t[0, :, part] = jnp.where(tm < n_tm - 1, value[0:E].astype(F32), 0.0).astype(BF16)
        edge_t[1, :, part] = jnp.where(tm > 0, value[E : 2 * E].astype(F32), 0.0).astype(BF16)
        in_t[2 * E :, part] = value[2 * E :]
    in_next = send(edge_t.at[0], in_t.at[pl.ds(0, E)], tm_next)
    in_prev = send(edge_t.at[1], in_t.at[pl.ds(E, E)], tm_prev)
    og_t[...] = og[...].T
    grad = dot(og_t[...], h2o[...])
    halves(d0, grad[:, 0:M], 16, 64)
    bo[...] = grad[:, M:].reshape(16, 64, WP)
    bh[8:16] = as_column(mid)
    loads[4].wait()
    for r in range(BAND):
        h1p[r * WP : (r + 1) * WP, :] = pad_rows(h1_v[r].astype(F32))
    h1_t[...] = h1p[...].T
    halves(kf.at[pl.ds(6, 6)], dot(h1_t[...], m3[WP : WP + NP, :]), 16, 16)
    def slab(piece, t, low, s):
        if piece == 0 and s >= 4 or piece == 1:
            tap = s - 1 if piece == 0 else s if s < 3 else s + 3
            parts = [kf[2 * tap + h, t, pl.ds(low, 8, stride=2), :] for h in range(2)]
        elif piece == 0 or s != 2:
            held, j = (d0, s) if piece == 0 else (d2, s - s // 3)
            parts = [held[h, t, pl.ds(4 * low + j, 8, stride=8), :] for h in range(2)]
        else:
            lane = lax.broadcasted_iota(jnp.int32, (8, 128), 1)
            total = jnp.zeros((8, 128), F32)
            for j in range(4):
                total = jnp.where(lane == j, bo[t, pl.ds(4 * low + j, 8, stride=8), :], total)
            for j in range(2):
                total = jnp.where(lane == 4 + j, bh[t, pl.ds(2 * low + j, 8, stride=4), :], total)
            parts = [total, jnp.zeros((8, 128), F32)]
        return jnp.concatenate(parts, 0)

    def two_terms(value):
        total = value[0:8] + value[8:16]
        head = total.astype(BF16).astype(F32)
        return jnp.concatenate([head, total - head], 0)

    bufs = (
        (cs0, cr0, a1s0, a1r0, b1s0, b1r0, a2s0, a2r0, b2s0, b2r0, zf0, zs0, zr0),
        (cs1, cr1, a1s1, a1r1, b1s1, b1r1, a2s1, a2r1, b2s1, b2r1, zf1, zs1, zr1),
        (cs2, cr2, xys2, xyr2, None, None, None, None, None, None, zf2, zs2, zr2),
    )

    late3 = []

    def core_phase(p):
        na, nb = PIECES[p]
        cs, cr = bufs[p][:2]

        def body(x, carry):
            for y in range(4):
                t = ((y // 2) * 4 + x) * 2 + (1 - core)
                for s in range(na + nb):
                    value = slab(p, t, y % 2, s)
                    if p == 2 and s == 2:
                        value = two_terms(value)
                    cs[x, y, s] = value.astype(BF16)
            return carry

        lax.fori_loop(0, 4, body, 0)
        return [send(cs, cr, sibling)]

    def first_phase(p, copies):
        na, nb = PIECES[p]
        cs, cr, a1s, a1r, b1s, b1r = bufs[p][:6]
        for copy in copies:
            copy.wait()

        def body(x, carry):
            for y in range(4):
                t = ((y // 2) * 4 + x) * 2 + core
                for s in range(na + nb):
                    value = slab(p, t, y % 2, s) + cr[x, y, s].astype(F32)
                    if p == 2 and s == 2:
                        value = two_terms(value)
                    if p == 2 and s > 2:
                        for h in range(2):
                            row = x * 16 + y * 4 + 2 * (s - 3) + h
                            zf3[pl.ds(row, 8, stride=64), :] = value[8 * h : 8 * h + 8]
                    elif s < na:
                        a1s[x, y, s] = value.astype(BF16)
                    else:
                        b1s[y, x, s - na] = value.astype(BF16)
            return carry

        lax.fori_loop(0, 4, body, 0)
        out = []
        if p == 2:
            zs3[...] = zf3[...].reshape(8, 64, 128).astype(BF16)
            for k in (4, 3, 5, 2, 6, 1, 7):
                late3.append(send(zs3.at[(mz + k) % 8], zr3.at[k - 1], z_peer[k - 1]))
            for (i, j), peer in sorted(xy_peer.items(), key=lambda item: -(item[0][0] % 3 + item[0][1] % 3)):
                out.append(send(a1s.at[(mx + i) % 4, (my + j) % 4], a1r.at[4 * i + j - 1], peer))
            return out
        for k in (2, 1, 3):
            out.append(send(a1s.at[(mx + k) % 4], a1r.at[k - 1], x_peer[k - 1]))
            out.append(send(b1s.at[(my + k) % 4], b1r.at[k - 1], y_peer[k - 1]))
        return out

    def gathered(own, held, got, j):
        total = held[own, j].astype(F32)
        for k in range(3):
            total = total + got[k, j].astype(F32)
        return total

    def second_phase(p, copies):
        na, nb = PIECES[p]
        _, _, a1s, a1r, b1s, b1r, a2s, a2r, b2s, b2r = bufs[p][:10]
        for copy in copies:
            copy.wait()
        for j in range(4):
            a2s[j] = gathered(mx, a1s, a1r, j).astype(BF16)
            b2s[j] = gathered(my, b1s, b1r, j).astype(BF16)
        out = []
        for k in (2, 1, 3):
            out.append(send(a2s.at[(my + k) % 4], a2r.at[k - 1], y_peer[k - 1]))
            out.append(send(b2s.at[(mx + k) % 4], b2r.at[k - 1], x_peer[k - 1]))
        return out

    def third_phase(p, copies):
        na, nb = PIECES[p]
        _, _, xys, xyr, _, _, a2s, a2r, b2s, b2r, zf, zs, zr = bufs[p]
        for copy in copies:
            copy.wait()
        for s in range(3 if p == 2 else na + nb):
            if p == 2:
                total = xys[mx, my, s].astype(F32)
                for k in range(15):
                    total = total + xyr[k, s].astype(F32)
                if s == 2:
                    total = two_terms(total)
            else:
                own, held, got, j = (my, a2s, a2r, s) if s < na else (mx, b2s, b2r, s - na)
                total = gathered(own, held, got, j)
            for h in range(2):
                zf[pl.ds(2 * s + h, 8, stride=DEPTH), :] = total[8 * h : 8 * h + 8]
        zs[...] = zf[...].reshape(8, DEPTH, 128).astype(BF16)
        return [send(zs.at[(mz + k) % 8], zr.at[k - 1], z_peer[k - 1]) for k in (4, 3, 5, 2, 6, 1, 7)]

    def last_phase(p, copies, result):
        zf, _, zr = bufs[p][10:]
        for copy in copies:
            copy.wait()
        total = zf[pl.ds(pl.multiple_of(mz * DEPTH, 8), DEPTH), :]
        for k in range(7):
            total = total + zr[k].astype(F32)
        result[...] = total

    def cross_phase(copies):
        for copy in copies:
            copy.wait()
        total = zs3[mz].astype(F32)
        for k in range(7):
            total = total + zr3[k].astype(F32)
        sum3[0:64, :] = total
        for i in range(16):
            xys3[i] = sum3[4 * i : 4 * i + 8, :]
        out = []
        for (i, j), peer in sorted(xy_peer.items(), key=lambda item: -(item[0][0] % 3 + item[0][1] % 3)):
            out.append(send(xys3.at[((mx + i) % 4) * 4 + (my + j) % 4], xyr3.at[4 * i + j - 1], peer))
        return out

    def cross_end(copies, result):
        for copy in copies:
            copy.wait()
        total = xys3[mx * 4 + my]
        for k in range(15):
            total = total + xyr3[k]
        result[...] = total

    flight0 = core_phase(0)

    def back_of(start, count, a):
        total = None
        for b in range(3):
            term = dot_t1(m3[start : start + count, b * M : (b + 1) * M], wmid_v[a, b])
            total = term if total is None else total + term
        return total

    loads[6].wait()
    back[...] = back_of(WP, NP, 1)
    back[0 : NP - WP, :] += back_of(2 * WP, NP - WP, 0)
    back[WP:NP, :] += back_of(WP, NP - WP, 2)

    flight0 = first_phase(0, flight0)
    halves(kf.at[pl.ds(0, 6)], dot(h1_t[:, 0 : NP - WP], m3[2 * WP : WP + NP, :]), 16, 16)
    halves(kf.at[pl.ds(12, 6)], dot(h1_t[:, WP:NP], m3[WP:NP, :]), 16, 16)

    mid_down.wait()
    mid_up.wait()
    for held, start in ((mup, 0), (mdn, NP + WP)):
        value = held[...].astype(F32)
        m3[start : start + WP, 0:M] = pltpu.roll(value, WP - 1, 0).astype(BF16)
        m3[start : start + WP, M : 2 * M] = held[...]
        m3[start : start + WP, 2 * M : 3 * M] = pltpu.roll(value, 1, 0).astype(BF16)
    for first_tap, grad in (
        (0, dot(h1_t[:, NP - WP :], m3[NP + WP :, :])),
        (12, dot(h1_t[:, 0:WP], m3[0:WP, :])),
    ):
        for h in range(6):
            kf[first_tap + h] += grad[:, h * 128 : (h + 1) * 128].reshape(16, 16, 128)
    flight1 = core_phase(1)

    back[0:WP, :] += back_of(0, WP, 2)
    back[NP - WP : NP, :] += back_of(NP + WP, WP, 0)
    first_grad = jnp.where(h1p[...].astype(F32) > 0, back[...], 0.0).astype(BF16)
    first[...] = first_grad
    bh[0:8] = as_column(first_grad)
    in_next.wait()
    in_prev.wait()
    halves(d2, dot(in_t[...], first[...]), 16, 64)
    flight2 = core_phase(2)
    flight1 = first_phase(1, flight1)

    loads[7].wait()
    edge = dot_t1(first[...], win_v[0 : 2 * E, :])
    prod_e[...] = jnp.where(tm > 0, edge[:, 0:E], 0.0).astype(BF16)
    prod_l[...] = jnp.where(tm < n_tm - 1, edge[:, E:], 0.0).astype(BF16)
    early = send(prod_e, got_e, tm_prev)
    late = send(prod_l, got_l, tm_next)
    flight2 = first_phase(2, flight2)

    rest = og[:, 2 * E :].astype(F32) + dot_t1(first[...], win_v[2 * E :, :])
    for r in range(BAND):
        gi[r, :, 2 * E :] = rest[r * WP : r * WP + W].astype(BF16)
    flight0 = second_phase(0, flight0)
    flight1 = second_phase(1, flight1)
    flight0 = third_phase(0, flight0)
    early.wait()
    late.wait()
    for r in range(BAND):
        part = slice(r * WP, r * WP + WP)
        one = og[part, 0:E].astype(F32) + got_e[part, :].astype(F32)
        two = og[part, E : 2 * E].astype(F32) + got_l[part, :].astype(F32)
        gi[r, :, 0:E] = one[:W].astype(BF16)
        gi[r, :, E : 2 * E] = two[:W].astype(BF16)


    flight2 = third_phase(2, flight2)
    flight3 = cross_phase(late3)
    flight1 = third_phase(1, flight1)
    last_phase(0, flight0, f0_out)
    last_phase(2, flight2, f2_out)
    cross_end(flight3, f3_out)
    last_phase(1, flight1, f1_out)


def scratch():
    def v(*shape, dtype=BF16):
        return pltpu.VMEM(shape, dtype)

    shapes = [
        v(BAND, W, C), v(BAND, W, M), v(BAND, W, M), v(BAND, W, C), v(BAND, W, C),
        v(C, M), v(3, 3, M, M), v(M, C),
        v(NP, C), v(C, NP), v(NP, M + WP), v(NP, M), v(M, NP), v(NP + 2 * WP, 3 * M),
        v(C, NP), v(2, E, NP), v(NP, M), v(NP, M), v(2, WP, M), v(WP, M), v(WP, M),
        v(NP, E), v(NP, E), v(NP, E), v(NP, E),
        v(NP, M, dtype=F32), v(2, 16, 64, 128, dtype=F32), v(18, 16, 16, 128, dtype=F32), v(2, 16, 64, 128, dtype=F32),
        v(16, 64, WP, dtype=F32), v(16, 32, WP, dtype=F32),
    ]
    tile = (16, 128)
    for na, nb in PIECES:
        shapes += [v(4, 4, na + nb, *tile), v(4, 4, na + nb, *tile)]
        if nb:
            shapes += [v(4, 4, na, *tile), v(3, 4, na, *tile), v(4, 4, nb, *tile), v(3, 4, nb, *tile)]
            shapes += [v(4, na, *tile), v(3, na, *tile), v(4, nb, *tile), v(3, nb, *tile)]
        else:
            shapes += [v(4, 4, 3, *tile), v(15, 3, *tile)]
        shapes += [v(8 * DEPTH, 128, dtype=F32), v(8, DEPTH, 128), v(7, DEPTH, 128)]
    shapes += [v(8 * 64, 128, dtype=F32), v(8, 64, 128), v(7, 64, 128)]
    shapes += [v(72, 128, dtype=F32), v(16, 8, 128, dtype=F32), v(15, 8, 128, dtype=F32)]
    shapes += [pltpu.SemaphoreType.DMA((9,)), pltpu.SemaphoreType.DMA((100,)), pltpu.SemaphoreType.DMA((100,))]
    return shapes


def finish(
    held, f0, f1, f2, f3, gi, d_in, d_mid, d_out, b_hidden, b_out,
    d_in_v, d_mid_v, d_out_v, b_hidden_v, b_out_v, store_sem,
):
    results = [(d_in_v, d_in), (d_mid_v, d_mid), (d_out_v, d_out), (b_hidden_v, b_hidden), (b_out_v, b_out)]
    results = [(held.at[r], gi.at[r]) for r in range(BAND)] + results
    stores = [pltpu.make_async_copy(src, dst, store_sem.at[i]) for i, (src, dst) in enumerate(results)]

    def lines(ref, start, count):
        return jnp.concatenate([ref[pl.ds(2 * start + h, count, stride=2), :] for h in range(2)], 1)

    for store in stores[:BAND]:
        store.start()
    d_in_v[0:2, :] = lines(f2, 0, 2)
    d_in_v[2:4, :] = lines(f3, 0, 2)
    d_mid_v[0] = lines(f1, 0, 3)
    d_mid_v[1] = lines(f0, 4, 3)
    d_mid_v[2] = lines(f1, 3, 3)
    d_out_v[...] = lines(f0, 0, 4)
    bias = f2[4, :] + f2[5, :]
    b_hidden_v[...] = bias[4:6]
    b_out_v[...] = bias[0:4]
    for store in stores[BAND:]:
        store.start()
    for store in stores:
        store.wait()


def on_device(inputs, hidden_one, hidden_two, outputs, cotangent, w_in, w_mid, w_out):
    anywhere = pl.BlockSpec(memory_space=pl.ANY)
    vmem = pl.BlockSpec(memory_space=pltpu.VMEM)
    gi, f0, f1, f2, f3 = pl.pallas_call(
        kernel,
        out_shape=[
            pltpu.VMEM((BAND, W, C), BF16),
            pltpu.VMEM((DEPTH, 128), F32),
            pltpu.VMEM((DEPTH, 128), F32),
            pltpu.VMEM((DEPTH, 128), F32),
            pltpu.VMEM((8, 128), F32),
        ],
        in_specs=[anywhere] * 8,
        out_specs=[vmem] * 5,
        scratch_shapes=scratch(),
        compiler_params=pltpu.CompilerParams(
            collective_id=0, has_side_effects=True, vmem_limit_bytes=56 * 2**20
        ),
    )(inputs[0], hidden_one[0], hidden_two[0], outputs[0], cotangent[0], w_in, w_mid, w_out)
    gi, d_in, d_mid, d_out, b_hidden, b_out = pl.pallas_call(
        finish,
        out_shape=[
            jax.ShapeDtypeStruct((BAND, W, C), BF16),
            jax.ShapeDtypeStruct((4, M), F32),
            jax.ShapeDtypeStruct((3, 3, M), F32),
            jax.ShapeDtypeStruct((4, M), F32),
            jax.ShapeDtypeStruct((2,), F32),
            jax.ShapeDtypeStruct((4,), F32),
        ],
        in_specs=[vmem] * 5,
        out_specs=[anywhere] * 6,
        scratch_shapes=[
            pltpu.VMEM((4, M), F32),
            pltpu.VMEM((3, 3, M), F32),
            pltpu.VMEM((4, M), F32),
            pltpu.VMEM((2,), F32),
            pltpu.VMEM((4,), F32),
            pltpu.SemaphoreType.DMA((BAND + 5,)),
        ],
        compiler_params=pltpu.CompilerParams(vmem_limit_bytes=8 * 2**20),
    )(gi, f0, f1, f2, f3)
    return gi[None], d_in, d_mid, d_out.T, b_hidden, b_out


def solution(mesh):
    placed = (
        P("tm", "rows", None, None),
        P("tm", "rows", None, None),
        P("tm", "rows", None, None),
        P("tm", "rows", None, None),
        P("tm", "rows", None, None),
        P(),
        P(),
        P(),
    )
    return jax.shard_map(
        on_device,
        mesh=mesh,
        in_specs=placed,
        out_specs=(
            P("tm", "rows", None, None),
            P(("tm", "rows"), None),
            P(None, None, ("tm", "rows")),
            P(None, ("tm", "rows")),
            P(("tm", "rows")),
            P(("tm", "rows")),
        ),
        check_vma=False,
    )
```
